32 devices in a mesh: gy: 8 (over y, x, core), pa: 4 (over z).
Axes of the slice: x: 2, y: 2, z: 4, core: 2. Of those that a mesh axis runs over, the one named last changes fastest.
Arguments:
- spectral_velocity: float32 [3, 16, 512, 1536], P(None, 'gy', 'pa'), may hold values from -0.01913664 to 0.01913664
- inverse_spacing: float32 [16], P('gy'), may hold values from 0.25 to 1
Outputs:
- increment: float32 [3, 16, 1152, 1536], P(None, 'gy', 'pa')
- vorticity_peak: float32 [], replicated
The draws below stay inside these ranges and needn't reach their ends.
All inputs are finite; a program needn't handle non-finite values.
Results may differ from the reference program's by a relative error of at most 0.00011.
Values sent between devices are 32-bit elements; how exact they have to be, the bound alone decides.
A program may use at most 128 MiB of HBM per device.

```python
import math
import jax
import jax.numpy as jnp
from jax import lax

NX = 1536
NZ = 1152
KX = 512
KZ = 768
NY = 16


def draw_spectral_velocity(key, part):
    key_values, key_planes = jax.random.split(key, 2)
    shape = (3, NY, KX, 2 * KZ)
    base = 0.5 / jnp.sqrt(jnp.float32(KX * KZ))
    planes = jnp.arange(NY, dtype=jnp.float32)
    rising = 1.0 + 2.0 * planes / max(NY - 1, 1)
    jitter = jnp.exp(jax.random.uniform(key_planes, (NY,), jnp.float32, jnp.log(0.7), jnp.log(1.4)))
    amplitude = (rising * jitter)[None, :, None, None]
    raw = jnp.clip(jax.random.normal(key_values, shape, jnp.float32), -4.0, 4.0)
    values = raw * base * amplitude
    return jnp.clip(values, -24.0 * base, 24.0 * base)


def shard_levels(key, shape, pieces, low, top_value):
    factor_of, own = 1.0, jax.random.fold_in(key, 6)
    for axis_at, shards_of in pieces:
        steps = jnp.exp(jax.random.uniform(jax.random.fold_in(own, axis_at), (shards_of,), jnp.float32, low / len(pieces), top_value / len(pieces)))
        factor_of = factor_of * jnp.repeat(steps, shape[axis_at] // shards_of).reshape([-1 if axis == axis_at else 1 for axis in range(len(shape))])
    return factor_of


def setup_inputs(seed: int = 0) -> dict:
    seeds = jax.random.split(jax.random.key(seed), 3)
    return {
        "spectral_velocity": draw_spectral_velocity(jax.random.fold_in(seeds[2], 71), 0),
        "inverse_spacing": jnp.clip(jnp.exp(math.log(1.0) - 1.3862944 * jax.random.uniform(seeds[1], (NY,), jnp.float32) ** shard_levels(seeds[1], (NY,), ((0, 8),), -0.2, 0.2)), 0.25, 1.0),
    }


def synthesize(modes):
    column = jnp.arange(KZ, dtype=jnp.int32)
    target = jnp.where(column < KZ // 2, column, column + (NZ - KZ))
    spread = jnp.zeros((modes.shape[0], KX, NZ), dtype=modes.dtype).at[:, :, target].set(modes)
    along_z = jnp.fft.ifft(spread, axis=-1) * NZ
    weight = jnp.where(jnp.arange(KX, dtype=jnp.int32) == 0, 1.0, 2.0)
    padded = jnp.zeros((modes.shape[0], NZ, NX), dtype=modes.dtype)
    padded = padded.at[:, :, :KX].set(jnp.transpose(along_z, (0, 2, 1)) * weight)
    return jnp.real(jnp.fft.ifft(padded, axis=-1) * NX)

def complexify(block):
    return block[..., :KZ] + 1j * block[..., KZ:]

def reference(spectral_velocity, inverse_spacing):
    wave_x = (jnp.arange(KX, dtype=jnp.int32).astype(jnp.float32) * (2.0 * math.pi / NX))[:, None]
    column = jnp.arange(KZ, dtype=jnp.int32)
    wave_z = jnp.where(column < KZ // 2, column, column - KZ).astype(jnp.float32) * (2.0 * math.pi / NZ)
    padded = jnp.pad(spectral_velocity, ((0, 0), (1, 1), (0, 0), (0, 0)))
    pair = jnp.array([0, 2], dtype=jnp.int32)

    def one_plane(index):
        below = complexify(lax.dynamic_index_in_dim(padded, index, 1, keepdims=False))
        center = complexify(lax.dynamic_index_in_dim(padded, index + 1, 1, keepdims=False))
        above = complexify(lax.dynamic_index_in_dim(padded, index + 2, 1, keepdims=False))
        spectra = jnp.stack((center[0], center[1], center[2], 1j * wave_z * center[1], 1j * wave_z * center[0] - 1j * wave_x * center[2], 1j * wave_x * center[1]))
        fields = synthesize(spectra)
        lower = synthesize(below[pair])
        upper = synthesize(above[pair])
        scale = lax.dynamic_index_in_dim(inverse_spacing, index, 0, keepdims=False)
        dy_u = (upper[0] - lower[0]) * scale
        dy_w = (upper[1] - lower[1]) * scale
        vort_x = dy_w - fields[3]
        vort_y = fields[4]
        vort_z = fields[5] - dy_u
        lamb = jnp.stack((fields[1] * vort_z - fields[2] * vort_y, fields[2] * vort_x - fields[0] * vort_z, fields[0] * vort_y - fields[1] * vort_x))
        return (lamb, jnp.max(vort_x * vort_x + vort_y * vort_y + vort_z * vort_z))
    lamb, peaks = lax.map(one_plane, jnp.arange(NY, dtype=jnp.int32))
    peak = jnp.sqrt(jnp.max(peaks))
    return (jnp.transpose(lamb, (1, 0, 2, 3)) / (peak + 1e-06), peak)
```

```python
import functools
import math

import ml_dtypes
import numpy as np

import jax
import jax.numpy as jnp
from jax import lax
from jax.experimental import pallas as pl
from jax.experimental.pallas import tpu as pltpu
from jax.sharding import PartitionSpec as P

NX = 1536
NZ = 1152
KX = 512
MESH = pl.DeviceIdType.MESH
TILE = 256


def z_table(length, modes, parts):
    column = np.arange(modes)
    wave = np.where(column < modes // 2, column, column - modes)
    angles = (wave[None, :] * np.arange(length)[:, None] % length) * (2.0 * math.pi / length)
    cos, sin = np.cos(angles), np.sin(angles)
    scale = (wave * (2.0 * math.pi / length))[None, :]

    def lay(rr, ri, ir, ii):
        real = np.concatenate((rr, ri), 1).reshape(parts, 1, length // parts, 2 * modes)
        imag = np.concatenate((ir, ii), 1).reshape(parts, 1, length // parts, 2 * modes)
        both = np.concatenate((real, imag), 1)
        return both.reshape(parts, -1, 2 * modes).astype(np.float32)

    plain = lay(cos, -sin, sin, cos)
    slope = lay(-scale * sin, -scale * cos, scale * cos, -scale * sin)
    return plain, slope


def x_table(length, modes, parts):
    column = np.arange(modes)
    angles = (column[:, None] * np.arange(length)[None, :] % length) * (2.0 * math.pi / length)
    weight = np.where(column == 0, 1.0, 2.0)[:, None]
    both = np.stack((weight * np.cos(angles), -weight * np.sin(angles)))
    both = both.reshape(2, parts, modes // parts, length)
    return np.moveaxis(both, 1, 0).astype(np.float32)


def everywhere_max(value, axes):
    for axis in axes:
        count = lax.axis_size(axis)
        shift = 1
        while shift < count:
            pairs = [(i, (i + shift) % count) for i in range(count)]
            value = jnp.maximum(value, lax.ppermute(value, axis, pairs))
            shift *= 2
    return value


def plain_body(spectral_velocity, inverse_spacing):
    planes, kx_local, width = spectral_velocity.shape[1:]
    parts = lax.axis_size("pa")
    levels = lax.axis_size("gy")
    me = lax.axis_index("pa")
    slab = NZ // parts
    plain, slope = z_table(NZ, width // 2, parts)
    order = (me - jnp.arange(parts)) % parts
    pieces = x_table(NX, KX, parts)
    pieces = np.concatenate([pieces[[-k % parts]] for k in range(2 * parts)])
    pieces = np.ascontiguousarray(np.moveaxis(pieces, 1, 0)).reshape(2, -1, NX)
    table_x = lax.dynamic_slice_in_dim(
        jnp.asarray(pieces), (parts - me) * kx_local, KX, axis=1
    ).reshape(2 * KX, NX)
    kx = (order[:, None] * kx_local + jnp.arange(kx_local)[None, :]).reshape(-1)
    wave_x = kx.astype(jnp.float32) * (2.0 * math.pi / NX)

    def exchange(modes, table):
        out = jnp.einsum(
            "dnk,fjmk->dfjnm", table, modes, precision=lax.Precision.HIGH,
            preferred_element_type=jnp.float32,
        )
        got = [lax.dynamic_index_in_dim(out, me, 0, keepdims=False)]
        for shift in range(1, parts):
            block = lax.dynamic_index_in_dim(out, (me + shift) % parts, 0, keepdims=False)
            got.append(lax.ppermute(block, "pa", [(i, (i + shift) % parts) for i in range(parts)]))
        whole = jnp.concatenate(got, axis=-1)
        return whole.reshape(whole.shape[:2] + (2, slab, KX))

    def to_x(hat):
        flat = jnp.concatenate((hat[..., 0, :, :], hat[..., 1, :, :]), axis=-1)
        return jnp.einsum(
            "...zm,mx->...zx", flat, table_x, precision=lax.Precision.HIGH,
            preferred_element_type=jnp.float32,
        )

    def turned(hat):
        return jnp.stack((-wave_x * hat[..., 1, :, :], wave_x * hat[..., 0, :, :]), axis=-3)

    u_modes, v_modes, w_modes = (spectral_velocity[c : c + 1] for c in range(3))
    uw_hat = exchange(jnp.concatenate((u_modes, w_modes)), plain)
    dzu_hat = exchange(u_modes, slope)[0]
    v_hat = exchange(v_modes, plain)[0]
    dzv_hat = exchange(v_modes, slope)[0]

    below = lax.ppermute(uw_hat[:, -1:], "gy", [(i, i + 1) for i in range(levels - 1)])
    above = lax.ppermute(uw_hat[:, :1], "gy", [(i + 1, i) for i in range(levels - 1)])
    spacing = inverse_spacing[None, :, None, None, None]
    lower = jnp.concatenate((below, uw_hat[:, :-1]), axis=1)
    upper = jnp.concatenate((uw_hat[:, 1:], above), axis=1)
    slope_y = (upper - lower) * spacing

    u, w = to_x(uw_hat[0]), to_x(uw_hat[1])
    vort_y = to_x(dzu_hat - turned(uw_hat[1]))
    v = to_x(v_hat)
    vort_z = to_x(turned(v_hat) - slope_y[0])
    vort_x = to_x(slope_y[1] - dzv_hat)
    lamb = jnp.stack(
        (v * vort_z - w * vort_y, w * vort_x - u * vort_z, u * vort_y - v * vort_x)
    )
    local_peak = jnp.max(vort_x * vort_x + vort_y * vort_y + vort_z * vort_z)
    magnitude = jnp.sqrt(everywhere_max(local_peak, ("gy", "pa")))
    return (lamb / (magnitude + 1e-06), magnitude)


def halves(table):
    table = np.asarray(table, np.float32)
    high = table.astype(ml_dtypes.bfloat16)
    low = (table - high.astype(np.float32)).astype(ml_dtypes.bfloat16)
    return high, low


def z_factors(length, modes, parts):
    slab = length // parts
    half = slab // 2
    top = modes // 2
    middle = (slab - 1) / 2
    points = np.arange(half, slab) - middle
    wave = np.arange(top + 1)
    step = 2.0 * math.pi / length
    angle = step * np.outer(points, wave)
    share = wave / top
    even = np.concatenate((np.cos(angle), -share * np.sin(angle)))
    odd = np.concatenate((np.sin(angle), share * np.cos(angle)))
    left_e, size_e, _ = np.linalg.svd(even, full_matrices=False)
    left_o, size_o, _ = np.linalg.svd(odd, full_matrices=False)
    limit = 3e-8 * max(size_e[0], size_o[0])
    rank = max(int((size_e > limit).sum()), int((size_o > limit).sum()))
    rank = min(-(-rank // 4) * 4, size_e.size, size_o.size)
    left_e, left_o = left_e[:, :rank], left_o[:, :rank]
    value = np.concatenate((
        np.concatenate((left_e[:half][::-1], left_e[:half])),
        np.concatenate((-left_o[:half][::-1], left_o[:half])),
    ), 1)
    slope = np.concatenate((
        np.concatenate((-left_e[half:][::-1], left_e[half:])),
        np.concatenate((left_o[half:][::-1], left_o[half:])),
    ), 1) * (top * step)
    column = np.arange(modes)
    signed = np.where(column < top, column, column - modes)
    kernel = np.concatenate((
        (left_e.T @ even)[:, np.abs(signed)] + 0j,
        1j * np.sign(signed) * (left_o.T @ odd)[:, np.abs(signed)],
    ))
    centre = np.arange(parts) * slab + middle
    phase = np.exp(1j * step * np.outer(centre, signed))
    return np.concatenate((value, slope)), kernel[None] * phase[:, None, :]


def z_tables(length, modes, parts):
    expand, reduce = z_factors(length, modes, parts)
    rank = expand.shape[1]
    real = np.concatenate((reduce.real, -reduce.imag), 2)
    imag = np.concatenate((reduce.imag, reduce.real), 2)
    table = np.concatenate((real, imag), 1)
    reduce = np.concatenate(halves(table), 1)
    wide = np.zeros((expand.shape[0], -(-rank // TILE) * TILE), np.float32)
    wide[:, :rank] = expand
    return reduce, np.stack(halves(wide)), rank


def x_tables(length, modes):
    column = np.arange(modes)
    angle = (column[:, None] * np.arange(length)[None, :] % length) * (2.0 * math.pi / length)
    weight = np.where(column == 0, 1.0, 2.0)[:, None]
    return np.stack(halves(np.concatenate((weight * np.cos(angle), -weight * np.sin(angle)))))


def split(value):
    high = value.astype(jnp.bfloat16)
    return high, (value - high.astype(jnp.float32)).astype(jnp.bfloat16)


def dot(a, b):
    return jnp.dot(a, b, preferred_element_type=jnp.float32)


def field_kernel(
    parts, levels, rank, wave_ref, space_ref, x_hbm, reduce_hbm, expand_hbm, table_hbm,
    lamb_ref, peak_ref,
    x_ref, xt_ref, reduce_ref, expand_ref, table_ref, send, recv, halo, lhs, part_x, peaks,
    load_sem, send_sem, recv_sem, halo_send, halo_recv, peak_send, peak_recv,
):
    me, level = lax.axis_index("pa"), lax.axis_index("gy")
    planes, kx_local, width = x_ref.shape[1:]
    slab = lamb_ref.shape[2]
    two = 2 * rank
    tall = lhs.shape[0] // 4
    wide = expand_ref.shape[2]
    shifts = sorted(range(1, parts), key=lambda s: (abs(2 * s - parts), s))
    fields = (0, 2, 1)

    loads = {}

    def load(key, source, target):
        loads[key] = pltpu.make_async_copy(source, target, load_sem.at[len(loads)])
        loads[key].start()

    def slab_of(shift):
        return lax.rem(me + shift, parts)

    load(("x", 0), x_hbm.at[0], x_ref.at[0])
    for shift in shifts + [0]:
        load(("reduce", shift), reduce_hbm.at[slab_of(shift)], reduce_ref.at[shift])
    load(("x", 2), x_hbm.at[2], x_ref.at[2])
    load(("x", 1), x_hbm.at[1], x_ref.at[1])
    load("table", table_hbm, table_ref)
    load("expand", expand_hbm, expand_ref)

    @pl.when(level == 0)
    def _():
        halo[:, 0] = jnp.zeros_like(halo[:, 0])

    @pl.when(level == levels - 1)
    def _():
        halo[:, 1] = jnp.zeros_like(halo[:, 1])

    barrier = pltpu.get_barrier_semaphore()
    for shift in range(1, parts):
        pl.semaphore_signal(
            barrier, inc=1, device_id={"pa": slab_of(shift)}, device_id_type=MESH
        )
    for shift in range(1, levels):
        pl.semaphore_signal(
            barrier, inc=1, device_id={"gy": lax.rem(level + shift, levels)}, device_id_type=MESH
        )
    pl.semaphore_wait(barrier, parts + levels - 2)

    def transfer(f, j, shift):
        return pltpu.make_async_remote_copy(
            src_ref=send.at[f, j, shift - 1],
            dst_ref=recv.at[f, j, me],
            send_sem=send_sem.at[f, j, shift],
            recv_sem=recv_sem.at[f, j, shift],
            device_id={"pa": slab_of(shift)},
            device_id_type=MESH,
        )

    def arrive(f, j):
        for shift in shifts:
            transfer(f, j, shift).wait_recv()

    def reduce_field(f):
        loads["x", f].wait()

        @pl.loop(0, width // 128)
        def _(n):
            at = pl.ds(pl.multiple_of(n * 128, 128), 128)
            for j in range(planes):
                high, low = split(x_ref[f, j, :, at].T)
                lanes = slice(j * kx_local, (j + 1) * kx_local)
                xt_ref[0, at, lanes] = high
                xt_ref[1, at, lanes] = low

        for shift in shifts + [0]:
            if f == fields[0]:
                loads["reduce", shift].wait()
            both = dot(reduce_ref[shift], xt_ref[0])
            out = both[:two] + both[two:] + dot(reduce_ref[shift, :two, :], xt_ref[1])
            for j in range(planes):
                piece = out[:, j * kx_local : (j + 1) * kx_local]
                if shift:
                    send[f, j, shift - 1] = piece
                else:
                    recv[f, j, me] = piece
            if shift:
                for j in range(planes):
                    transfer(f, j, shift).start()

    def halo_copy(f, up):
        if up:
            return pltpu.make_async_remote_copy(
                src_ref=recv.at[f, planes - 1], dst_ref=halo.at[f // 2, 0],
                send_sem=halo_send.at[f // 2, 0], recv_sem=halo_recv.at[f // 2, 0],
                device_id={"gy": lax.rem(level + 1, levels)}, device_id_type=MESH,
            )
        return pltpu.make_async_remote_copy(
            src_ref=recv.at[f, 0], dst_ref=halo.at[f // 2, 1],
            send_sem=halo_send.at[f // 2, 1], recv_sem=halo_recv.at[f // 2, 1],
            device_id={"gy": lax.rem(level + levels - 1, levels)}, device_id_type=MESH,
        )

    def halo_start(f):
        @pl.when(level < levels - 1)
        def _():
            halo_copy(f, True).start()

        @pl.when(level > 0)
        def _():
            halo_copy(f, False).start()

    def halo_arrive(f):
        @pl.when(level > 0)
        def _():
            halo_copy(f, True).wait_recv()

        @pl.when(level < levels - 1)
        def _():
            halo_copy(f, False).wait_recv()

    def halo_sent(f):
        @pl.when(level < levels - 1)
        def _():
            halo_copy(f, True).wait_send()

        @pl.when(level > 0)
        def _():
            halo_copy(f, False).wait_send()

    def fill(slot, hat):
        @pl.loop(0, parts)
        def _(source):
            here = pl.multiple_of(source * kx_local, kx_local)
            for c in range(2):
                value = hat(source, here, c)
                if tall > rank:
                    value = jnp.concatenate((value, jnp.zeros((tall - rank, kx_local), jnp.float32)))
                high, low = split(value)
                lanes = pl.ds(pl.multiple_of(c * KX + here, kx_local), kx_local)
                lhs[slot * tall : (slot + 1) * tall, lanes] = high
                lhs[(2 + slot) * tall : (3 + slot) * tall, lanes] = low

    def half(c):
        return slice(c * rank, (c + 1) * rank)

    def modes(f, j):
        return lambda source, here, c: recv[f, j, source, half(c), :]

    def turned(f, j):
        def hat(source, here, c):
            wave = wave_ref[0:1, pl.ds(here, kx_local)]
            other = recv[f, j, source, half(1 - c), :] * wave
            return other if c else -other
        return hat

    def slope_y(f, j):
        def hat(source, here, c):
            lower = halo[f // 2, 0, source, half(c), :] if j == 0 else recv[f, j - 1, source, half(c), :]
            upper = (
                halo[f // 2, 1, source, half(c), :] if j == planes - 1
                else recv[f, j + 1, source, half(c), :]
            )
            return (upper - lower) * space_ref[j]
        return hat

    def minus(first, second):
        return lambda source, here, c: first(source, here, c) - second(source, here, c)

    def to_x(at):
        both = dot(lhs[...], table_ref[0, :, at])
        out = both[: 2 * tall] + both[2 * tall :] + dot(lhs[: 2 * tall, :], table_ref[1, :, at])
        return out[:tall], out[tall:]

    def to_z(value, rows):
        if wide > tall:
            value = jnp.concatenate((value, jnp.zeros((wide - tall, TILE), jnp.float32)))
        high, low = split(value)
        return (
            dot(expand_ref[0, :rows, :], high)
            + dot(expand_ref[1, :rows, :], high)
            + dot(expand_ref[0, :rows, :], low)
        )

    def tiles(step, init):
        def at_tile(t, carry):
            return step(pl.ds(pl.multiple_of(t * TILE, TILE), TILE), carry)
        return lax.fori_loop(0, NX // TILE, at_tile, init)

    for f in fields:
        reduce_field(f)
    loads["table"].wait()
    loads["expand"].wait()

    for j in range(planes):
        arrive(0, j)
    halo_start(0)
    for j in range(planes):
        fill(j, modes(0, j))

    def u_tile(at, carry):
        for j, value in enumerate(to_x(at)):
            both = to_z(value, 2 * slab)
            lamb_ref[0, j, :, at] = both[:slab]
            lamb_ref[2, j, :, at] = both[slab:]
        return carry

    tiles(u_tile, 0)

    for j in range(planes):
        arrive(2, j)
    halo_start(2)
    for j in range(planes):
        fill(0, modes(2, j))
        fill(1, turned(2, j))

        def w_tile(at, carry):
            w, dx_w = to_x(at)
            lamb_ref[1, j, :, at] = to_z(w, slab)
            lamb_ref[2, j, :, at] = lamb_ref[2, j, :, at] - to_z(dx_w, slab)
            return carry

        tiles(w_tile, 0)

    halo_arrive(0)
    halo_arrive(2)
    for j in range(planes):
        fill(j, slope_y(2, j))

    def dy_tile(at, carry):
        for j, value in enumerate(to_x(at)):
            part_x[j, :, at] = to_z(value, slab)
        return carry

    tiles(dy_tile, 0)

    top = jnp.zeros((8, TILE), jnp.float32)
    for j in range(planes):
        arrive(1, j)
        fill(0, modes(1, j))
        fill(1, minus(turned(1, j), slope_y(0, j)))

        def v_tile(at, top):
            v, vort_z = to_x(at)
            v = to_z(v, 2 * slab)
            vort_z = to_z(vort_z, slab)
            vort_x = part_x[j, :, at] - v[slab:]
            v = v[:slab]
            u, w, vort_y = lamb_ref[0, j, :, at], lamb_ref[1, j, :, at], lamb_ref[2, j, :, at]
            lamb_ref[0, j, :, at] = v * vort_z - w * vort_y
            lamb_ref[1, j, :, at] = w * vort_x - u * vort_z
            lamb_ref[2, j, :, at] = u * vort_y - v * vort_x
            square = vort_x * vort_x + vort_y * vort_y + vort_z * vort_z
            return jnp.maximum(top, square.reshape(slab // 8, 8, TILE).max(0))

        top = tiles(v_tile, top)

    def peak_copy(axis, count, base, here, shift):
        return pltpu.make_async_remote_copy(
            src_ref=peaks.at[base], dst_ref=peaks.at[base + shift],
            send_sem=peak_send.at[base + shift], recv_sem=peak_recv.at[base + shift],
            device_id={axis: lax.rem(here + shift, count)}, device_id_type=MESH,
        )

    value = top[:, :128]
    for k in range(1, TILE // 128):
        value = jnp.maximum(value, top[:, k * 128 : (k + 1) * 128])
    base = 0
    for axis, count, here in (("gy", levels, level), ("pa", parts, me)):
        peaks[base] = value
        copies = [peak_copy(axis, count, base, here, shift) for shift in range(1, count)]
        for copy in copies:
            copy.start()
        for copy in copies:
            copy.wait()
        for shift in range(1, count):
            value = jnp.maximum(value, peaks[base + shift])
        base += count
    peak = jnp.sqrt(jnp.max(value, axis=(0, 1), keepdims=True))
    peak_ref[0] = jnp.broadcast_to(peak, value.shape)
    peak_ref[1] = jnp.broadcast_to(1.0 / (peak + 1e-06), value.shape)

    for f in fields:
        for j in range(planes):
            for shift in shifts:
                transfer(f, j, shift).wait_send()
    halo_sent(0)
    halo_sent(2)


def body(spectral_velocity, inverse_spacing):
    planes, kx_local, width = spectral_velocity.shape[1:]
    parts, levels = lax.axis_size("pa"), lax.axis_size("gy")
    slab = NZ // parts
    if planes != 2 or kx_local % 128 or slab % 16 or parts < 2 or levels < 2:
        return plain_body(spectral_velocity, inverse_spacing)
    reduce, expand, rank = z_tables(NZ, width // 2, parts)
    table = x_tables(NX, KX)
    wave = np.tile((np.arange(KX) * (2.0 * math.pi / NX)).astype(np.float32), (8, 1))
    tall = -(-rank // 16) * 16
    hbm = pl.BlockSpec(memory_space=pl.ANY)
    vmem = pl.BlockSpec(memory_space=pltpu.VMEM)
    block = (parts, 2 * rank, kx_local)
    dma = pltpu.SemaphoreType.DMA
    lamb, peak = pl.pallas_call(
        functools.partial(field_kernel, parts, levels, rank),
        out_shape=(
            jax.ShapeDtypeStruct((3, planes, slab, NX), jnp.float32),
            jax.ShapeDtypeStruct((2, 8, 128), jnp.float32),
        ),
        in_specs=[vmem, pl.BlockSpec(memory_space=pltpu.SMEM), hbm, hbm, hbm, hbm],
        out_specs=(vmem, vmem),
        scratch_shapes=[
            pltpu.VMEM((3, planes, kx_local, width), jnp.float32),
            pltpu.VMEM((2, width, planes * kx_local), jnp.bfloat16),
            pltpu.VMEM(reduce.shape, jnp.bfloat16),
            pltpu.VMEM(expand.shape, jnp.bfloat16),
            pltpu.VMEM(table.shape, jnp.bfloat16),
            pltpu.VMEM((3, planes, parts - 1) + block[1:], jnp.float32),
            pltpu.VMEM((3, planes) + block, jnp.float32),
            pltpu.VMEM((2, 2) + block, jnp.float32),
            pltpu.VMEM((4 * tall, 2 * KX), jnp.bfloat16),
            pltpu.VMEM((planes, slab, NX), jnp.float32),
            pltpu.VMEM((parts + levels, 8, 128), jnp.float32),
            dma((parts + 5,)),
            dma((3, planes, parts)),
            dma((3, planes, parts)),
            dma((2, 2)),
            dma((2, 2)),
            dma((parts + levels,)),
            dma((parts + levels,)),
        ],
        compiler_params=pltpu.CompilerParams(
            collective_id=0, has_side_effects=True, vmem_limit_bytes=62 * 2**20
        ),
    )(wave, inverse_spacing, spectral_velocity, reduce, expand, table)
    return lamb * peak[1, 0, 0], peak[0, 0, 0]


def solution(mesh):
    placed = (P(None, "gy", "pa", None), P("gy"))
    return jax.shard_map(
        body,
        mesh=mesh,
        in_specs=placed,
        out_specs=(P(None, "gy", "pa", None), P()),
        check_vma=False,
    )
```

```python
import functools
import math

import ml_dtypes
import numpy as np

import jax
import jax.numpy as jnp
from jax import lax
from jax.experimental import pallas as pl
from jax.experimental.pallas import tpu as pltpu
from jax.sharding import PartitionSpec as P

NX = 1536
NZ = 1152
KX = 512
MESH = pl.DeviceIdType.MESH
TILE = 256


def z_table(length, modes, parts):
    column = np.arange(modes)
    wave = np.where(column < modes // 2, column, column - modes)
    angles = (wave[None, :] * np.arange(length)[:, None] % length) * (2.0 * math.pi / length)
    cos, sin = np.cos(angles), np.sin(angles)
    scale = (wave * (2.0 * math.pi / length))[None, :]

    def lay(rr, ri, ir, ii):
        real = np.concatenate((rr, ri), 1).reshape(parts, 1, length // parts, 2 * modes)
        imag = np.concatenate((ir, ii), 1).reshape(parts, 1, length // parts, 2 * modes)
        both = np.concatenate((real, imag), 1)
        return both.reshape(parts, -1, 2 * modes).astype(np.float32)

    plain = lay(cos, -sin, sin, cos)
    slope = lay(-scale * sin, -scale * cos, scale * cos, -scale * sin)
    return plain, slope


def x_table(length, modes, parts):
    column = np.arange(modes)
    angles = (column[:, None] * np.arange(length)[None, :] % length) * (2.0 * math.pi / length)
    weight = np.where(column == 0, 1.0, 2.0)[:, None]
    both = np.stack((weight * np.cos(angles), -weight * np.sin(angles)))
    both = both.reshape(2, parts, modes // parts, length)
    return np.moveaxis(both, 1, 0).astype(np.float32)


def everywhere_max(value, axes):
    for axis in axes:
        count = lax.axis_size(axis)
        shift = 1
        while shift < count:
            pairs = [(i, (i + shift) % count) for i in range(count)]
            value = jnp.maximum(value, lax.ppermute(value, axis, pairs))
            shift *= 2
    return value


def plain_body(spectral_velocity, inverse_spacing):
    planes, kx_local, width = spectral_velocity.shape[1:]
    parts = lax.axis_size("pa")
    levels = lax.axis_size("gy")
    me = lax.axis_index("pa")
    slab = NZ // parts
    plain, slope = z_table(NZ, width // 2, parts)
    order = (me - jnp.arange(parts)) % parts
    pieces = x_table(NX, KX, parts)
    pieces = np.concatenate([pieces[[-k % parts]] for k in range(2 * parts)])
    pieces = np.ascontiguousarray(np.moveaxis(pieces, 1, 0)).reshape(2, -1, NX)
    table_x = lax.dynamic_slice_in_dim(
        jnp.asarray(pieces), (parts - me) * kx_local, KX, axis=1
    ).reshape(2 * KX, NX)
    kx = (order[:, None] * kx_local + jnp.arange(kx_local)[None, :]).reshape(-1)
    wave_x = kx.astype(jnp.float32) * (2.0 * math.pi / NX)

    def exchange(modes, table):
        out = jnp.einsum(
            "dnk,fjmk->dfjnm", table, modes, precision=lax.Precision.HIGH,
            preferred_element_type=jnp.float32,
        )
        got = [lax.dynamic_index_in_dim(out, me, 0, keepdims=False)]
        for shift in range(1, parts):
            block = lax.dynamic_index_in_dim(out, (me + shift) % parts, 0, keepdims=False)
            got.append(lax.ppermute(block, "pa", [(i, (i + shift) % parts) for i in range(parts)]))
        whole = jnp.concatenate(got, axis=-1)
        return whole.reshape(whole.shape[:2] + (2, slab, KX))

    def to_x(hat):
        flat = jnp.concatenate((hat[..., 0, :, :], hat[..., 1, :, :]), axis=-1)
        return jnp.einsum(
            "...zm,mx->...zx", flat, table_x, precision=lax.Precision.HIGH,
            preferred_element_type=jnp.float32,
        )

    def turned(hat):
        return jnp.stack((-wave_x * hat[..., 1, :, :], wave_x * hat[..., 0, :, :]), axis=-3)

    u_modes, v_modes, w_modes = (spectral_velocity[c : c + 1] for c in range(3))
    uw_hat = exchange(jnp.concatenate((u_modes, w_modes)), plain)
    dzu_hat = exchange(u_modes, slope)[0]
    v_hat = exchange(v_modes, plain)[0]
    dzv_hat = exchange(v_modes, slope)[0]

    below = lax.ppermute(uw_hat[:, -1:], "gy", [(i, i + 1) for i in range(levels - 1)])
    above = lax.ppermute(uw_hat[:, :1], "gy", [(i + 1, i) for i in range(levels - 1)])
    spacing = inverse_spacing[None, :, None, None, None]
    lower = jnp.concatenate((below, uw_hat[:, :-1]), axis=1)
    upper = jnp.concatenate((uw_hat[:, 1:], above), axis=1)
    slope_y = (upper - lower) * spacing

    u, w = to_x(uw_hat[0]), to_x(uw_hat[1])
    vort_y = to_x(dzu_hat - turned(uw_hat[1]))
    v = to_x(v_hat)
    vort_z = to_x(turned(v_hat) - slope_y[0])
    vort_x = to_x(slope_y[1] - dzv_hat)
    lamb = jnp.stack(
        (v * vort_z - w * vort_y, w * vort_x - u * vort_z, u * vort_y - v * vort_x)
    )
    local_peak = jnp.max(vort_x * vort_x + vort_y * vort_y + vort_z * vort_z)
    magnitude = jnp.sqrt(everywhere_max(local_peak, ("gy", "pa")))
    return (lamb / (magnitude + 1e-06), magnitude)


def halves(table):
    table = np.asarray(table, np.float32)
    high = table.astype(ml_dtypes.bfloat16)
    low = (table - high.astype(np.float32)).astype(ml_dtypes.bfloat16)
    return high, low


def z_factors(length, modes, parts):
    slab = length // parts
    half = slab // 2
    top = modes // 2
    middle = (slab - 1) / 2
    points = np.arange(half, slab) - middle
    wave = np.arange(top + 1)
    step = 2.0 * math.pi / length
    angle = step * np.outer(points, wave)
    share = wave / top
    even = np.concatenate((np.cos(angle), -share * np.sin(angle)))
    odd = np.concatenate((np.sin(angle), share * np.cos(angle)))
    left_e, size_e, _ = np.linalg.svd(even, full_matrices=False)
    left_o, size_o, _ = np.linalg.svd(odd, full_matrices=False)
    limit = 3e-8 * max(size_e[0], size_o[0])
    rank = max(int((size_e > limit).sum()), int((size_o > limit).sum()))
    rank = min(-(-rank // 4) * 4, size_e.size, size_o.size)
    left_e, left_o = left_e[:, :rank], left_o[:, :rank]
    value = np.concatenate((
        np.concatenate((left_e[:half][::-1], left_e[:half])),
        np.concatenate((-left_o[:half][::-1], left_o[:half])),
    ), 1)
    slope = np.concatenate((
        np.concatenate((-left_e[half:][::-1], left_e[half:])),
        np.concatenate((left_o[half:][::-1], left_o[half:])),
    ), 1) * (top * step)
    column = np.arange(modes)
    signed = np.where(column < top, column, column - modes)
    kernel = np.concatenate((
        (left_e.T @ even)[:, np.abs(signed)] + 0j,
        1j * np.sign(signed) * (left_o.T @ odd)[:, np.abs(signed)],
    ))
    centre = np.arange(parts) * slab + middle
    phase = np.exp(1j * step * np.outer(centre, signed))
    return np.concatenate((value, slope)), kernel[None] * phase[:, None, :]


def z_tables(length, modes, parts):
    expand, reduce = z_factors(length, modes, parts)
    rank = expand.shape[1]
    real = np.concatenate((reduce.real, -reduce.imag), 2)
    imag = np.concatenate((reduce.imag, reduce.real), 2)
    table = np.concatenate((real, imag), 1)
    reduce = np.concatenate(halves(table), 1)
    wide = np.zeros((expand.shape[0], -(-rank // TILE) * TILE), np.float32)
    wide[:, :rank] = expand
    return reduce, np.stack(halves(wide)), rank


def x_tables(length, modes, parts):
    own = modes // parts
    column = np.arange(modes).reshape(parts, own // 2, 2).transpose(2, 0, 1)[:, :, None, :]
    step = 2.0 * math.pi / length
    angle = (column[..., None] * np.arange(length // 2) % length) * step
    weight = np.where(column == 0, 1.0, 2.0)[..., None]
    table = np.concatenate((weight * np.cos(angle), -weight * np.sin(angle)), 2)
    wave = np.concatenate((-step * column, step * column), 2).reshape(2, 1, modes)
    return (
        np.stack(halves(table.reshape(2, modes, length // 2))),
        np.tile(wave.astype(np.float32), (1, 8, 1)),
    )


def split(value):
    high = value.astype(jnp.bfloat16)
    return high, (value - high.astype(jnp.float32)).astype(jnp.bfloat16)


def dot(a, b):
    return jnp.dot(a, b, preferred_element_type=jnp.float32)


def field_kernel(
    parts, levels, rank, wave_ref, space_ref, x_hbm, reduce_hbm, expand_hbm, table_hbm,
    lamb_ref, peak_ref,
    x_ref, xt_ref, reduce_ref, expand_ref, table_ref, send, recv, halo, lhs, part_x, peaks, tile,
    load_sem, send_sem, recv_sem, halo_send, halo_recv, peak_send, peak_recv,
):
    me, level = lax.axis_index("pa"), lax.axis_index("gy")
    planes, kx_local, width = x_ref.shape[1:]
    slab = lamb_ref.shape[2]
    two = 2 * rank
    tall = lhs.shape[0] // 4
    wide = expand_ref.shape[2]
    shifts = sorted(range(1, parts), key=lambda s: (abs(2 * s - parts), s))
    fields = (0, 2, 1)

    loads = {}

    def load(key, source, target):
        loads[key] = pltpu.make_async_copy(source, target, load_sem.at[len(loads)])
        loads[key].start()

    def slab_of(shift):
        return lax.rem(me + shift, parts)

    load(("x", 0), x_hbm.at[0], x_ref.at[0])
    for shift in shifts + [0]:
        load(("reduce", shift), reduce_hbm.at[slab_of(shift)], reduce_ref.at[shift])
    load(("x", 2), x_hbm.at[2], x_ref.at[2])
    load(("x", 1), x_hbm.at[1], x_ref.at[1])
    load("table", table_hbm, table_ref)
    load("expand", expand_hbm, expand_ref)

    @pl.when(level == 0)
    def _():
        halo[:, 0] = jnp.zeros_like(halo[:, 0])

    @pl.when(level == levels - 1)
    def _():
        halo[:, 1] = jnp.zeros_like(halo[:, 1])

    barrier = pltpu.get_barrier_semaphore()
    for shift in range(1, parts):
        pl.semaphore_signal(
            barrier, inc=1, device_id={"pa": slab_of(shift)}, device_id_type=MESH
        )
    for shift in range(1, levels):
        pl.semaphore_signal(
            barrier, inc=1, device_id={"gy": lax.rem(level + shift, levels)}, device_id_type=MESH
        )
    pl.semaphore_wait(barrier, parts + levels - 2)

    def transfer(f, j, shift):
        return pltpu.make_async_remote_copy(
            src_ref=send.at[f, j, shift - 1],
            dst_ref=recv.at[f, j, me],
            send_sem=send_sem.at[f, j, shift],
            recv_sem=recv_sem.at[f, j, shift],
            device_id={"pa": slab_of(shift)},
            device_id_type=MESH,
        )

    def arrive(f, j):
        for shift in shifts:
            transfer(f, j, shift).wait_recv()

    def reduce_field(f):
        loads["x", f].wait()

        @pl.loop(0, width // 128)
        def _(n):
            at = pl.ds(pl.multiple_of(n * 128, 128), 128)
            for j in range(planes):
                tile[j] = x_ref[f, j, :, at]
                rows = jnp.concatenate((
                    tile[j, pl.ds(0, kx_local // 2, stride=2), :],
                    tile[j, pl.ds(1, kx_local // 2, stride=2), :],
                ))
                high, low = split(rows.T)
                lanes = slice(j * kx_local, (j + 1) * kx_local)
                xt_ref[0, at, lanes] = high
                xt_ref[1, at, lanes] = low

        for shift in shifts + [0]:
            if f == fields[0]:
                loads["reduce", shift].wait()
            both = dot(reduce_ref[shift], xt_ref[0])
            out = both[:two] + both[two:] + dot(reduce_ref[shift, :two, :], xt_ref[1])
            for j in range(planes):
                real = out[:rank, j * kx_local : (j + 1) * kx_local]
                imag = out[rank:, j * kx_local : (j + 1) * kx_local]
                first = lax.broadcasted_iota(jnp.int32, real.shape, 1) < kx_local // 2
                even = jnp.where(first, real, pltpu.roll(imag, kx_local // 2, 1))
                odd = jnp.where(first, pltpu.roll(real, kx_local // 2, 1), imag)
                if shift:
                    send[f, j, shift - 1, half(0), :] = even
                    send[f, j, shift - 1, half(1), :] = odd
                else:
                    recv[f, j, me, half(0), :] = even
                    recv[f, j, me, half(1), :] = odd
            if shift and f == fields[0]:
                for j in range(planes):
                    transfer(f, j, shift).start()

    def follow(f, before):
        for j in range(planes):
            for shift in shifts:
                transfer(before, j, shift).wait_send()
                transfer(f, j, shift).start()

    def halo_copy(f, up):
        if up:
            return pltpu.make_async_remote_copy(
                src_ref=recv.at[f, planes - 1], dst_ref=halo.at[f // 2, 0],
                send_sem=halo_send.at[f // 2, 0], recv_sem=halo_recv.at[f // 2, 0],
                device_id={"gy": lax.rem(level + 1, levels)}, device_id_type=MESH,
            )
        return pltpu.make_async_remote_copy(
            src_ref=recv.at[f, 0], dst_ref=halo.at[f // 2, 1],
            send_sem=halo_send.at[f // 2, 1], recv_sem=halo_recv.at[f // 2, 1],
            device_id={"gy": lax.rem(level + levels - 1, levels)}, device_id_type=MESH,
        )

    def halo_start(f):
        @pl.when(level < levels - 1)
        def _():
            halo_copy(f, True).start()

        @pl.when(level > 0)
        def _():
            halo_copy(f, False).start()

    def halo_arrive(f):
        @pl.when(level > 0)
        def _():
            halo_copy(f, True).wait_recv()

        @pl.when(level < levels - 1)
        def _():
            halo_copy(f, False).wait_recv()

    def halo_sent(f):
        @pl.when(level < levels - 1)
        def _():
            halo_copy(f, True).wait_send()

        @pl.when(level > 0)
        def _():
            halo_copy(f, False).wait_send()

    def fill(slot, hat):
        @pl.loop(0, parts)
        def _(source):
            here = pl.multiple_of(source * kx_local, kx_local)
            for c in range(2):
                value = hat(source, here, c)
                if tall > rank:
                    value = jnp.concatenate((value, jnp.zeros((tall - rank, kx_local), jnp.float32)))
                high, low = split(value)
                lanes = pl.ds(pl.multiple_of(c * KX + here, kx_local), kx_local)
                lhs[slot * tall : (slot + 1) * tall, lanes] = high
                lhs[(2 + slot) * tall : (3 + slot) * tall, lanes] = low

    def half(c):
        return slice(c * rank, (c + 1) * rank)

    def modes(f, j):
        return lambda source, here, c: recv[f, j, source, half(c), :]

    def turned(f, j):
        def hat(source, here, c):
            wave = wave_ref[c, 0:1, pl.ds(here, kx_local)]
            return pltpu.roll(recv[f, j, source, half(c), :], kx_local // 2, 1) * wave
        return hat

    def slope_y(f, j):
        def hat(source, here, c):
            lower = halo[f // 2, 0, source, half(c), :] if j == 0 else recv[f, j - 1, source, half(c), :]
            upper = (
                halo[f // 2, 1, source, half(c), :] if j == planes - 1
                else recv[f, j + 1, source, half(c), :]
            )
            return (upper - lower) * space_ref[j]
        return hat

    def minus(first, second):
        return lambda source, here, c: first(source, here, c) - second(source, here, c)

    def to_x(at):
        def of(c):
            lanes = slice(c * KX, (c + 1) * KX)
            both = dot(lhs[:, lanes], table_ref[0, c, :, at])
            return both[: 2 * tall] + both[2 * tall :] + dot(lhs[: 2 * tall, lanes], table_ref[1, c, :, at])

        even, odd = of(0), of(1)
        out = jnp.concatenate((even + odd, even - odd), 1)
        return out[:tall], out[tall:]

    def to_z(value, rows):
        if wide > tall:
            value = jnp.concatenate((value, jnp.zeros((wide - tall, 2 * TILE), jnp.float32)))
        high, low = split(value)
        return (
            dot(expand_ref[0, :rows, :], high)
            + dot(expand_ref[1, :rows, :], high)
            + dot(expand_ref[0, :rows, :], low)
        )

    def tiles(step, init):
        def at_tile(t, carry):
            at = pl.ds(pl.multiple_of(t * TILE, TILE), TILE)
            far = pl.ds(pl.multiple_of(NX // 2 + t * TILE, TILE), TILE)
            return step(at, ((slice(0, TILE), at), (slice(TILE, 2 * TILE), far)), carry)
        return lax.fori_loop(0, NX // 2 // TILE, at_tile, init)

    for f in fields:
        reduce_field(f)
    loads["table"].wait()
    loads["expand"].wait()

    follow(2, 0)
    for j in range(planes):
        arrive(0, j)
    halo_start(0)
    for j in range(planes):
        fill(j, modes(0, j))

    def u_tile(at, sides, carry):
        for j, value in enumerate(to_x(at)):
            both = to_z(value, 2 * slab)
            for part, to in sides:
                lamb_ref[0, j, :, to] = both[:slab, part]
                lamb_ref[2, j, :, to] = both[slab:, part]
        return carry

    tiles(u_tile, 0)

    follow(1, 2)
    for j in range(planes):
        arrive(2, j)
    halo_start(2)
    for j in range(planes):
        fill(0, modes(2, j))
        fill(1, turned(2, j))

        def w_tile(at, sides, carry):
            w, dx_w = to_x(at)
            w, dx_w = to_z(w, slab), to_z(dx_w, slab)
            for part, to in sides:
                lamb_ref[1, j, :, to] = w[:, part]
                lamb_ref[2, j, :, to] = lamb_ref[2, j, :, to] - dx_w[:, part]
            return carry

        tiles(w_tile, 0)

    halo_arrive(0)
    halo_arrive(2)
    for j in range(planes):
        fill(j, slope_y(2, j))

    def dy_tile(at, sides, carry):
        for j, value in enumerate(to_x(at)):
            value = to_z(value, slab)
            for part, to in sides:
                part_x[j, :, to] = value[:, part]
        return carry

    tiles(dy_tile, 0)

    top = jnp.zeros((8, TILE), jnp.float32)
    for j in range(planes):
        arrive(1, j)
        fill(0, modes(1, j))
        fill(1, minus(turned(1, j), slope_y(0, j)))

        def v_tile(at, sides, top):
            value, turn = to_x(at)
            value = to_z(value, 2 * slab)
            turn = to_z(turn, slab)
            for part, to in sides:
                v, vort_z = value[:slab, part], turn[:, part]
                vort_x = part_x[j, :, to] - value[slab:, part]
                u, w, vort_y = lamb_ref[0, j, :, to], lamb_ref[1, j, :, to], lamb_ref[2, j, :, to]
                lamb_ref[0, j, :, to] = v * vort_z - w * vort_y
                lamb_ref[1, j, :, to] = w * vort_x - u * vort_z
                lamb_ref[2, j, :, to] = u * vort_y - v * vort_x
                square = vort_x * vort_x + vort_y * vort_y + vort_z * vort_z
                top = jnp.maximum(top, square.reshape(slab // 8, 8, TILE).max(0))
            return top

        top = tiles(v_tile, top)

    def peak_copy(axis, count, base, here, shift):
        return pltpu.make_async_remote_copy(
            src_ref=peaks.at[base], dst_ref=peaks.at[base + shift],
            send_sem=peak_send.at[base + shift], recv_sem=peak_recv.at[base + shift],
            device_id={axis: lax.rem(here + shift, count)}, device_id_type=MESH,
        )

    value = top[:, :128]
    for k in range(1, TILE // 128):
        value = jnp.maximum(value, top[:, k * 128 : (k + 1) * 128])
    base = 0
    for axis, count, here in (("gy", levels, level), ("pa", parts, me)):
        peaks[base] = value
        copies = [peak_copy(axis, count, base, here, shift) for shift in range(1, count)]
        for copy in copies:
            copy.start()
        for copy in copies:
            copy.wait()
        for shift in range(1, count):
            value = jnp.maximum(value, peaks[base + shift])
        base += count
    peak = jnp.sqrt(jnp.max(value, axis=(0, 1), keepdims=True))
    scale = 1.0 / (peak + 1e-06)

    @pl.loop(0, slab // 16)
    def _(n):
        rows = pl.ds(pl.multiple_of(n * 16, 16), 16)
        for c in range(3):
            for j in range(planes):
                lamb_ref[c, j, rows, :] = lamb_ref[c, j, rows, :] * scale

    peak_ref[...] = jnp.broadcast_to(peak, peak_ref.shape)

    for j in range(planes):
        for shift in shifts:
            transfer(1, j, shift).wait_send()
    halo_sent(0)
    halo_sent(2)


def body(spectral_velocity, inverse_spacing):
    planes, kx_local, width = spectral_velocity.shape[1:]
    parts, levels = lax.axis_size("pa"), lax.axis_size("gy")
    slab = NZ // parts
    if planes != 2 or kx_local % 128 or slab % 16 or parts < 2 or levels < 2:
        return plain_body(spectral_velocity, inverse_spacing)
    reduce, expand, rank = z_tables(NZ, width // 2, parts)
    table, wave = x_tables(NX, KX, parts)
    tall = -(-rank // 16) * 16
    hbm = pl.BlockSpec(memory_space=pl.ANY)
    vmem = pl.BlockSpec(memory_space=pltpu.VMEM)
    block = (parts, 2 * rank, kx_local)
    dma = pltpu.SemaphoreType.DMA
    lamb, peak = pl.pallas_call(
        functools.partial(field_kernel, parts, levels, rank),
        out_shape=(
            pltpu.VMEM((3, planes, slab, NX), jnp.float32),
            jax.ShapeDtypeStruct((8, 128), jnp.float32),
        ),
        in_specs=[vmem, pl.BlockSpec(memory_space=pltpu.SMEM), hbm, hbm, hbm, hbm],
        out_specs=(vmem, vmem),
        scratch_shapes=[
            pltpu.VMEM((3, planes, kx_local, width), jnp.float32),
            pltpu.VMEM((2, width, planes * kx_local), jnp.bfloat16),
            pltpu.VMEM(reduce.shape, jnp.bfloat16),
            pltpu.VMEM(expand.shape, jnp.bfloat16),
            pltpu.VMEM(table.shape, jnp.bfloat16),
            pltpu.VMEM((3, planes, parts - 1) + block[1:], jnp.float32),
            pltpu.VMEM((3, planes) + block, jnp.float32),
            pltpu.VMEM((2, 2) + block, jnp.float32),
            pltpu.VMEM((4 * tall, 2 * KX), jnp.bfloat16),
            pltpu.VMEM((planes, slab, NX), jnp.float32),
            pltpu.VMEM((parts + levels, 8, 128), jnp.float32),
            pltpu.VMEM((planes, kx_local, 128), jnp.float32),
            dma((parts + 5,)),
            dma((3, planes, parts)),
            dma((3, planes, parts)),
            dma((2, 2)),
            dma((2, 2)),
            dma((parts + levels,)),
            dma((parts + levels,)),
        ],
        compiler_params=pltpu.CompilerParams(
            collective_id=0, has_side_effects=True, vmem_limit_bytes=51 * 2**20
        ),
    )(wave, inverse_spacing, spectral_velocity, reduce, expand, table)
    return lamb, peak[0, 0]


def solution(mesh):
    placed = (P(None, "gy", "pa", None), P("gy"))
    return jax.shard_map(
        body,
        mesh=mesh,
        in_specs=placed,
        out_specs=(P(None, "gy", "pa", None), P()),
        check_vma=False,
    )
```

```python
import functools
import math

import ml_dtypes
import numpy as np

import jax
import jax.numpy as jnp
from jax import lax
from jax.experimental import pallas as pl
from jax.experimental.pallas import tpu as pltpu
from jax.sharding import PartitionSpec as P

NX = 1536
NZ = 1152
KX = 512
MESH = pl.DeviceIdType.MESH
TILE = 256


def z_table(length, modes, parts):
    column = np.arange(modes)
    wave = np.where(column < modes // 2, column, column - modes)
    angles = (wave[None, :] * np.arange(length)[:, None] % length) * (2.0 * math.pi / length)
    cos, sin = np.cos(angles), np.sin(angles)
    scale = (wave * (2.0 * math.pi / length))[None, :]

    def lay(rr, ri, ir, ii):
        real = np.concatenate((rr, ri), 1).reshape(parts, 1, length // parts, 2 * modes)
        imag = np.concatenate((ir, ii), 1).reshape(parts, 1, length // parts, 2 * modes)
        both = np.concatenate((real, imag), 1)
        return both.reshape(parts, -1, 2 * modes).astype(np.float32)

    plain = lay(cos, -sin, sin, cos)
    slope = lay(-scale * sin, -scale * cos, scale * cos, -scale * sin)
    return plain, slope


def x_table(length, modes, parts):
    column = np.arange(modes)
    angles = (column[:, None] * np.arange(length)[None, :] % length) * (2.0 * math.pi / length)
    weight = np.where(column == 0, 1.0, 2.0)[:, None]
    both = np.stack((weight * np.cos(angles), -weight * np.sin(angles)))
    both = both.reshape(2, parts, modes // parts, length)
    return np.moveaxis(both, 1, 0).astype(np.float32)


def everywhere_max(value, axes):
    for axis in axes:
        count = lax.axis_size(axis)
        shift = 1
        while shift < count:
            pairs = [(i, (i + shift) % count) for i in range(count)]
            value = jnp.maximum(value, lax.ppermute(value, axis, pairs))
            shift *= 2
    return value


def plain_body(spectral_velocity, inverse_spacing):
    planes, kx_local, width = spectral_velocity.shape[1:]
    parts = lax.axis_size("pa")
    levels = lax.axis_size("gy")
    me = lax.axis_index("pa")
    slab = NZ // parts
    plain, slope = z_table(NZ, width // 2, parts)
    order = (me - jnp.arange(parts)) % parts
    pieces = x_table(NX, KX, parts)
    pieces = np.concatenate([pieces[[-k % parts]] for k in range(2 * parts)])
    pieces = np.ascontiguousarray(np.moveaxis(pieces, 1, 0)).reshape(2, -1, NX)
    table_x = lax.dynamic_slice_in_dim(
        jnp.asarray(pieces), (parts - me) * kx_local, KX, axis=1
    ).reshape(2 * KX, NX)
    kx = (order[:, None] * kx_local + jnp.arange(kx_local)[None, :]).reshape(-1)
    wave_x = kx.astype(jnp.float32) * (2.0 * math.pi / NX)

    def exchange(modes, table):
        out = jnp.einsum(
            "dnk,fjmk->dfjnm", table, modes, precision=lax.Precision.HIGH,
            preferred_element_type=jnp.float32,
        )
        got = [lax.dynamic_index_in_dim(out, me, 0, keepdims=False)]
        for shift in range(1, parts):
            block = lax.dynamic_index_in_dim(out, (me + shift) % parts, 0, keepdims=False)
            got.append(lax.ppermute(block, "pa", [(i, (i + shift) % parts) for i in range(parts)]))
        whole = jnp.concatenate(got, axis=-1)
        return whole.reshape(whole.shape[:2] + (2, slab, KX))

    def to_x(hat):
        flat = jnp.concatenate((hat[..., 0, :, :], hat[..., 1, :, :]), axis=-1)
        return jnp.einsum(
            "...zm,mx->...zx", flat, table_x, precision=lax.Precision.HIGH,
            preferred_element_type=jnp.float32,
        )

    def turned(hat):
        return jnp.stack((-wave_x * hat[..., 1, :, :], wave_x * hat[..., 0, :, :]), axis=-3)

    u_modes, v_modes, w_modes = (spectral_velocity[c : c + 1] for c in range(3))
    uw_hat = exchange(jnp.concatenate((u_modes, w_modes)), plain)
    dzu_hat = exchange(u_modes, slope)[0]
    v_hat = exchange(v_modes, plain)[0]
    dzv_hat = exchange(v_modes, slope)[0]

    below = lax.ppermute(uw_hat[:, -1:], "gy", [(i, i + 1) for i in range(levels - 1)])
    above = lax.ppermute(uw_hat[:, :1], "gy", [(i + 1, i) for i in range(levels - 1)])
    spacing = inverse_spacing[None, :, None, None, None]
    lower = jnp.concatenate((below, uw_hat[:, :-1]), axis=1)
    upper = jnp.concatenate((uw_hat[:, 1:], above), axis=1)
    slope_y = (upper - lower) * spacing

    u, w = to_x(uw_hat[0]), to_x(uw_hat[1])
    vort_y = to_x(dzu_hat - turned(uw_hat[1]))
    v = to_x(v_hat)
    vort_z = to_x(turned(v_hat) - slope_y[0])
    vort_x = to_x(slope_y[1] - dzv_hat)
    lamb = jnp.stack(
        (v * vort_z - w * vort_y, w * vort_x - u * vort_z, u * vort_y - v * vort_x)
    )
    local_peak = jnp.max(vort_x * vort_x + vort_y * vort_y + vort_z * vort_z)
    magnitude = jnp.sqrt(everywhere_max(local_peak, ("gy", "pa")))
    return (lamb / (magnitude + 1e-06), magnitude)


def halves(table):
    table = np.asarray(table, np.float32)
    high = table.astype(ml_dtypes.bfloat16)
    low = (table - high.astype(np.float32)).astype(ml_dtypes.bfloat16)
    return high, low


def z_factors(length, modes, parts):
    slab = length // parts
    half = slab // 2
    top = modes // 2
    middle = (slab - 1) / 2
    points = np.arange(half, slab) - middle
    wave = np.arange(top + 1)
    step = 2.0 * math.pi / length
    angle = step * np.outer(points, wave)
    share = wave / top
    even = np.concatenate((np.cos(angle), -share * np.sin(angle)))
    odd = np.concatenate((np.sin(angle), share * np.cos(angle)))
    left_e, size_e, _ = np.linalg.svd(even, full_matrices=False)
    left_o, size_o, _ = np.linalg.svd(odd, full_matrices=False)
    limit = 3e-8 * max(size_e[0], size_o[0])
    rank = max(int((size_e > limit).sum()), int((size_o > limit).sum()))
    rank = min(-(-rank // 4) * 4, size_e.size, size_o.size)
    left_e, left_o = left_e[:, :rank], left_o[:, :rank]
    value = np.concatenate((
        np.concatenate((left_e[:half][::-1], left_e[:half])),
        np.concatenate((-left_o[:half][::-1], left_o[:half])),
    ), 1)
    slope = np.concatenate((
        np.concatenate((-left_e[half:][::-1], left_e[half:])),
        np.concatenate((left_o[half:][::-1], left_o[half:])),
    ), 1) * (top * step)
    column = np.arange(modes)
    signed = np.where(column < top, column, column - modes)
    kernel = np.concatenate((
        (left_e.T @ even)[:, np.abs(signed)] + 0j,
        1j * np.sign(signed) * (left_o.T @ odd)[:, np.abs(signed)],
    ))
    centre = np.arange(parts) * slab + middle
    phase = np.exp(1j * step * np.outer(centre, signed))
    return np.concatenate((value, slope)), kernel[None] * phase[:, None, :]


def z_tables(length, modes, parts):
    expand, reduce = z_factors(length, modes, parts)
    rank = expand.shape[1]
    real = np.concatenate((reduce.real, -reduce.imag), 2)
    imag = np.concatenate((reduce.imag, reduce.real), 2)
    table = np.concatenate((real, imag), 1)
    reduce = np.concatenate(halves(table), 1)
    wide = np.zeros((expand.shape[0], -(-rank // TILE) * TILE), np.float32)
    wide[:, :rank] = expand
    return reduce, np.stack(halves(wide)), rank


def x_tables(length, modes, parts):
    own = modes // parts
    column = np.arange(modes).reshape(parts, own // 2, 2).transpose(2, 0, 1)[:, :, None, :]
    step = 2.0 * math.pi / length
    angle = (column[..., None] * np.arange(length // 2) % length) * step
    weight = np.where(column == 0, 1.0, 2.0)[..., None]
    table = np.concatenate((weight * np.cos(angle), -weight * np.sin(angle)), 2)
    wave = np.concatenate((-step * column, step * column), 2).reshape(2, 1, modes)
    return (
        np.stack(halves(table.reshape(2, modes, length // 2))),
        np.tile(wave.astype(np.float32), (1, 8, 1)),
    )


def split(value):
    high = value.astype(jnp.bfloat16)
    return high, (value - high.astype(jnp.float32)).astype(jnp.bfloat16)


def dot(a, b):
    return jnp.dot(a, b, preferred_element_type=jnp.float32)


def field_kernel(
    parts, levels, rank, wave_ref, space_ref, x_hbm, reduce_hbm, expand_hbm, table_hbm,
    lamb_ref, peak_ref,
    x_ref, xt_ref, reduce_ref, expand_ref, table_ref, send, recv, halo, lhs, part_x, peaks, tile,
    load_sem, send_sem, recv_sem, halo_send, halo_recv, peak_send, peak_recv,
):
    me, level = lax.axis_index("pa"), lax.axis_index("gy")
    planes, kx_local, width = x_ref.shape[1:]
    slab = lamb_ref.shape[2]
    two = 2 * rank
    tall = lhs.shape[0] // 4
    wide = expand_ref.shape[2]
    shifts = sorted(range(1, parts), key=lambda s: (abs(2 * s - parts), s))
    fields = (2, 0, 1)

    loads = {}

    def load(key, source, target):
        loads[key] = pltpu.make_async_copy(source, target, load_sem.at[len(loads)])
        loads[key].start()

    def slab_of(shift):
        return lax.rem(me + shift, parts)

    def rest():
        for shift in shifts[1:] + [0]:
            load(("reduce", shift), reduce_hbm.at[slab_of(shift)], reduce_ref.at[shift])
        for f in fields[1:]:
            load(("x", f), x_hbm.at[f], x_ref.at[f])
        load("table", table_hbm, table_ref)
        load("expand", expand_hbm, expand_ref)

    first = fields[0]
    load(("x", first, 0), x_hbm.at[first, 0], x_ref.at[first, 0])
    load(("reduce", shifts[0]), reduce_hbm.at[slab_of(shifts[0])], reduce_ref.at[shifts[0]])
    for j in range(1, planes):
        load(("x", first, j), x_hbm.at[first, j], x_ref.at[first, j])

    @pl.when(level == 0)
    def _():
        halo[:, 0] = jnp.zeros_like(halo[:, 0])

    @pl.when(level == levels - 1)
    def _():
        halo[:, 1] = jnp.zeros_like(halo[:, 1])

    barrier = pltpu.get_barrier_semaphore()
    others = [(a, b) for a in range(levels) for b in range(parts) if a or b]

    def other(a, b):
        return {"gy": lax.rem(level + a, levels), "pa": lax.rem(me + b, parts)}

    for a, b in others:
        pl.semaphore_signal(barrier, inc=1, device_id=other(a, b), device_id_type=MESH)

    def transfer(f, j, shift):
        return pltpu.make_async_remote_copy(
            src_ref=send.at[f, j, shift - 1],
            dst_ref=recv.at[f, j, me],
            send_sem=send_sem.at[f, j, shift],
            recv_sem=recv_sem.at[f, j, shift],
            device_id={"pa": slab_of(shift)},
            device_id_type=MESH,
        )

    def arrive(f, j):
        for shift in shifts:
            transfer(f, j, shift).wait_recv()
            if f in (0, 2):
                halo_start(f, j, shift)

    def turn_modes(f, j):
        lanes = slice(j * kx_local, (j + 1) * kx_local)

        @pl.loop(0, width // 128)
        def _(n):
            at = pl.ds(pl.multiple_of(n * 128, 128), 128)
            tile[j] = x_ref[f, j, :, at]
            rows = jnp.concatenate((
                tile[j, pl.ds(0, kx_local // 2, stride=2), :],
                tile[j, pl.ds(1, kx_local // 2, stride=2), :],
            ))
            high, low = split(rows.T)
            xt_ref[0, at, lanes] = high
            xt_ref[1, at, lanes] = low

    def reduce_slab(f, shift, which):
        lanes = slice(which[0] * kx_local, (which[-1] + 1) * kx_local)
        both = dot(reduce_ref[shift], xt_ref[0, :, lanes])
        out = both[:two] + both[two:] + dot(reduce_ref[shift, :two, :], xt_ref[1, :, lanes])
        for n, j in enumerate(which):
            real = out[:rank, n * kx_local : (n + 1) * kx_local]
            imag = out[rank:, n * kx_local : (n + 1) * kx_local]
            left = lax.broadcasted_iota(jnp.int32, real.shape, 1) < kx_local // 2
            even = jnp.where(left, real, pltpu.roll(imag, kx_local // 2, 1))
            odd = jnp.where(left, pltpu.roll(real, kx_local // 2, 1), imag)
            if shift:
                send[f, j, shift - 1, half(0), :] = even
                send[f, j, shift - 1, half(1), :] = odd
            else:
                recv[f, j, me, half(0), :] = even
                recv[f, j, me, half(1), :] = odd

    def reduce_first(f):
        for j in range(planes):
            loads["x", f, j].wait()
            if j == planes - 1:
                rest()
            turn_modes(f, j)
            if j == 0:
                loads["reduce", shifts[0]].wait()
            reduce_slab(f, shifts[0], (j,))
            if j == 0:
                pl.semaphore_wait(barrier, len(others))
            transfer(f, j, shifts[0]).start()
        for shift in shifts[1:] + [0]:
            loads["reduce", shift].wait()
            reduce_slab(f, shift, range(planes))
            for j in range(planes):
                if shift:
                    transfer(f, j, shift).start()
                else:
                    halo_start(f, j, 0)

    def reduce_field(f):
        loads["x", f].wait()
        for j in range(planes):
            turn_modes(f, j)
        for shift in shifts + [0]:
            reduce_slab(f, shift, range(planes))
        if f == 0:
            for j in range(planes):
                halo_start(f, j, 0)

    def follow(f, j, before, k):
        for shift in shifts:
            transfer(before, k, shift).wait_send()
            transfer(f, j, shift).start()

    def halo_copy(f, up, shift):
        source = lax.rem(me + parts - shift, parts)
        side, j, step = (0, planes - 1, 1) if up else (1, 0, levels - 1)
        return pltpu.make_async_remote_copy(
            src_ref=recv.at[f, j, source], dst_ref=halo.at[f // 2, side, source],
            send_sem=halo_send.at[f // 2, side, shift], recv_sem=halo_recv.at[f // 2, side, shift],
            device_id={"gy": lax.rem(level + step, levels)}, device_id_type=MESH,
        )

    def halo_start(f, j, shift):
        @pl.when(level < levels - 1 if j else level > 0)
        def _():
            halo_copy(f, j > 0, shift).start()

    def halo_arrive(f):
        @pl.when(level > 0)
        def _():
            for shift in range(parts):
                halo_copy(f, True, shift).wait_recv()

        @pl.when(level < levels - 1)
        def _():
            for shift in range(parts):
                halo_copy(f, False, shift).wait_recv()

    def halo_sent(f):
        @pl.when(level < levels - 1)
        def _():
            for shift in range(parts):
                halo_copy(f, True, shift).wait_send()

        @pl.when(level > 0)
        def _():
            for shift in range(parts):
                halo_copy(f, False, shift).wait_send()

    def fill(slot, hat):
        @pl.loop(0, parts)
        def _(source):
            here = pl.multiple_of(source * kx_local, kx_local)
            for c in range(2):
                value = hat(source, here, c)
                if tall > rank:
                    value = jnp.concatenate((value, jnp.zeros((tall - rank, kx_local), jnp.float32)))
                high, low = split(value)
                lanes = pl.ds(pl.multiple_of(c * KX + here, kx_local), kx_local)
                lhs[slot * tall : (slot + 1) * tall, lanes] = high
                lhs[(2 + slot) * tall : (3 + slot) * tall, lanes] = low

    def half(c):
        return slice(c * rank, (c + 1) * rank)

    def modes(f, j):
        return lambda source, here, c: recv[f, j, source, half(c), :]

    def turned(f, j):
        def hat(source, here, c):
            wave = wave_ref[c, 0:1, pl.ds(here, kx_local)]
            return pltpu.roll(recv[f, j, source, half(c), :], kx_local // 2, 1) * wave
        return hat

    def slope_y(f, j):
        def hat(source, here, c):
            lower = halo[f // 2, 0, source, half(c), :] if j == 0 else recv[f, j - 1, source, half(c), :]
            upper = (
                halo[f // 2, 1, source, half(c), :] if j == planes - 1
                else recv[f, j + 1, source, half(c), :]
            )
            return (upper - lower) * space_ref[j]
        return hat

    def minus(first, second):
        return lambda source, here, c: first(source, here, c) - second(source, here, c)

    def to_x(at):
        def of(c):
            lanes = slice(c * KX, (c + 1) * KX)
            both = dot(lhs[:, lanes], table_ref[0, c, :, at])
            return both[: 2 * tall] + both[2 * tall :] + dot(lhs[: 2 * tall, lanes], table_ref[1, c, :, at])

        even, odd = of(0), of(1)
        out = jnp.concatenate((even + odd, even - odd), 1)
        return out[:tall], out[tall:]

    def to_z(value, rows):
        if wide > tall:
            value = jnp.concatenate((value, jnp.zeros((wide - tall, 2 * TILE), jnp.float32)))
        high, low = split(value)
        return (
            dot(expand_ref[0, :rows, :], high)
            + dot(expand_ref[1, :rows, :], high)
            + dot(expand_ref[0, :rows, :], low)
        )

    def tiles(step, init):
        def at_tile(t, carry):
            at = pl.ds(pl.multiple_of(t * TILE, TILE), TILE)
            far = pl.ds(pl.multiple_of(NX // 2 + t * TILE, TILE), TILE)
            return step(at, ((slice(0, TILE), at), (slice(TILE, 2 * TILE), far)), carry)
        return lax.fori_loop(0, NX // 2 // TILE, at_tile, init)

    reduce_first(first)
    for f in fields[1:]:
        reduce_field(f)
    loads["table"].wait()
    loads["expand"].wait()

    for j in range(planes):
        follow(0, j, 2, j)
    for j in range(planes):
        arrive(2, j)
    for j in range(planes):
        fill(0, modes(2, j))
        fill(1, turned(2, j))

        def w_tile(at, sides, carry):
            w, dx_w = to_x(at)
            w, dx_w = to_z(w, slab), to_z(dx_w, slab)
            for part, to in sides:
                lamb_ref[1, j, :, to] = w[:, part]
                lamb_ref[2, j, :, to] = dx_w[:, part]
            return carry

        tiles(w_tile, 0)

    arrive(0, 0)
    halo_arrive(2)
    for j in range(planes):
        fill(j, slope_y(2, j))

    def dy_tile(at, sides, carry):
        for j, value in enumerate(to_x(at)):
            value = to_z(value, slab)
            for part, to in sides:
                part_x[j, :, to] = value[:, part]
        return carry

    tiles(dy_tile, 0)

    follow(1, 0, 0, 1)
    for shift in shifts:
        transfer(0, 0, shift).wait_send()
        transfer(1, 1, shift).start()
    arrive(0, 1)
    for j in range(planes):
        fill(j, modes(0, j))

    def u_tile(at, sides, carry):
        for j, value in enumerate(to_x(at)):
            both = to_z(value, 2 * slab)
            for part, to in sides:
                lamb_ref[0, j, :, to] = both[:slab, part]
                lamb_ref[2, j, :, to] = both[slab:, part] - lamb_ref[2, j, :, to]
        return carry

    tiles(u_tile, 0)
    halo_arrive(0)

    top = jnp.zeros((8, TILE), jnp.float32)
    for j in range(planes):
        arrive(1, j)
        fill(0, modes(1, j))
        fill(1, minus(turned(1, j), slope_y(0, j)))

        def v_tile(at, sides, top):
            value, turn = to_x(at)
            value = to_z(value, 2 * slab)
            turn = to_z(turn, slab)
            for part, to in sides:
                v, vort_z = value[:slab, part], turn[:, part]
                vort_x = part_x[j, :, to] - value[slab:, part]
                u, w, vort_y = lamb_ref[0, j, :, to], lamb_ref[1, j, :, to], lamb_ref[2, j, :, to]
                lamb_ref[0, j, :, to] = v * vort_z - w * vort_y
                lamb_ref[1, j, :, to] = w * vort_x - u * vort_z
                lamb_ref[2, j, :, to] = u * vort_y - v * vort_x
                square = vort_x * vort_x + vort_y * vort_y + vort_z * vort_z
                top = jnp.maximum(top, square.reshape(slab // 8, 8, TILE).max(0))
            return top

        top = tiles(v_tile, top)

    value = top[:, :128]
    for k in range(1, TILE // 128):
        value = jnp.maximum(value, top[:, k * 128 : (k + 1) * 128])
    peaks[0] = value
    copies = [
        pltpu.make_async_remote_copy(
            src_ref=peaks.at[0], dst_ref=peaks.at[n + 1],
            send_sem=peak_send.at[n], recv_sem=peak_recv.at[n],
            device_id=other(a, b), device_id_type=MESH,
        )
        for n, (a, b) in enumerate(others)
    ]
    for copy in copies:
        copy.start()
    for copy in copies:
        copy.wait_recv()
    value = peaks[...].max(0)
    peak = jnp.sqrt(jnp.max(value, axis=(0, 1), keepdims=True))
    scale = 1.0 / (peak + 1e-06)

    @pl.loop(0, slab // 16)
    def _(n):
        rows = pl.ds(pl.multiple_of(n * 16, 16), 16)
        for c in range(3):
            for j in range(planes):
                lamb_ref[c, j, rows, :] = lamb_ref[c, j, rows, :] * scale

    peak_ref[...] = peak

    for j in range(planes):
        for shift in shifts:
            transfer(1, j, shift).wait_send()
    halo_sent(0)
    halo_sent(2)
    for copy in copies:
        copy.wait_send()


def body(spectral_velocity, inverse_spacing):
    planes, kx_local, width = spectral_velocity.shape[1:]
    parts, levels = lax.axis_size("pa"), lax.axis_size("gy")
    slab = NZ // parts
    if planes != 2 or kx_local % 128 or slab % 16 or parts < 2 or levels < 2:
        return plain_body(spectral_velocity, inverse_spacing)
    reduce, expand, rank = z_tables(NZ, width // 2, parts)
    table, wave = x_tables(NX, KX, parts)
    tall = -(-rank // 16) * 16
    hbm = pl.BlockSpec(memory_space=pl.ANY)
    vmem = pl.BlockSpec(memory_space=pltpu.VMEM)
    block = (parts, 2 * rank, kx_local)
    dma = pltpu.SemaphoreType.DMA
    lamb, peak = pl.pallas_call(
        functools.partial(field_kernel, parts, levels, rank),
        out_shape=(
            pltpu.VMEM((3, planes, slab, NX), jnp.float32),
            jax.ShapeDtypeStruct((1, 1), jnp.float32),
        ),
        in_specs=[vmem, pl.BlockSpec(memory_space=pltpu.SMEM), hbm, hbm, hbm, hbm],
        out_specs=(vmem, vmem),
        scratch_shapes=[
            pltpu.VMEM((3, planes, kx_local, width), jnp.float32),
            pltpu.VMEM((2, width, planes * kx_local), jnp.bfloat16),
            pltpu.VMEM(reduce.shape, jnp.bfloat16),
            pltpu.VMEM(expand.shape, jnp.bfloat16),
            pltpu.VMEM(table.shape, jnp.bfloat16),
            pltpu.VMEM((3, planes, parts - 1) + block[1:], jnp.float32),
            pltpu.VMEM((3, planes) + block, jnp.float32),
            pltpu.VMEM((2, 2) + block, jnp.float32),
            pltpu.VMEM((4 * tall, 2 * KX), jnp.bfloat16),
            pltpu.VMEM((planes, slab, NX), jnp.float32),
            pltpu.VMEM((parts * levels, 8, 128), jnp.float32),
            pltpu.VMEM((planes, kx_local, 128), jnp.float32),
            dma((parts + 6,)),
            dma((3, planes, parts)),
            dma((3, planes, parts)),
            dma((2, 2, parts)),
            dma((2, 2, parts)),
            dma((parts * levels - 1,)),
            dma((parts * levels - 1,)),
        ],
        compiler_params=pltpu.CompilerParams(
            collective_id=0, has_side_effects=True, vmem_limit_bytes=51 * 2**20
        ),
    )(wave, inverse_spacing, spectral_velocity, reduce, expand, table)
    return lamb, peak[0, 0]


def solution(mesh):
    placed = (P(None, "gy", "pa", None), P("gy"))
    return jax.shard_map(
        body,
        mesh=mesh,
        in_specs=placed,
        out_specs=(P(None, "gy", "pa", None), P()),
        check_vma=False,
    )
```

```python
import functools
import math

import ml_dtypes
import numpy as np

import jax
import jax.numpy as jnp
from jax import lax
from jax.experimental import pallas as pl
from jax.experimental.pallas import tpu as pltpu
from jax.sharding import PartitionSpec as P

NX = 1536
NZ = 1152
KX = 512
MESH = pl.DeviceIdType.MESH
TILE = 256


def z_table(length, modes, parts):
    column = np.arange(modes)
    wave = np.where(column < modes // 2, column, column - modes)
    angles = (wave[None, :] * np.arange(length)[:, None] % length) * (2.0 * math.pi / length)
    cos, sin = np.cos(angles), np.sin(angles)
    scale = (wave * (2.0 * math.pi / length))[None, :]

    def lay(rr, ri, ir, ii):
        real = np.concatenate((rr, ri), 1).reshape(parts, 1, length // parts, 2 * modes)
        imag = np.concatenate((ir, ii), 1).reshape(parts, 1, length // parts, 2 * modes)
        both = np.concatenate((real, imag), 1)
        return both.reshape(parts, -1, 2 * modes).astype(np.float32)

    plain = lay(cos, -sin, sin, cos)
    slope = lay(-scale * sin, -scale * cos, scale * cos, -scale * sin)
    return plain, slope


def x_table(length, modes, parts):
    column = np.arange(modes)
    angles = (column[:, None] * np.arange(length)[None, :] % length) * (2.0 * math.pi / length)
    weight = np.where(column == 0, 1.0, 2.0)[:, None]
    both = np.stack((weight * np.cos(angles), -weight * np.sin(angles)))
    both = both.reshape(2, parts, modes // parts, length)
    return np.moveaxis(both, 1, 0).astype(np.float32)


def everywhere_max(value, axes):
    for axis in axes:
        count = lax.axis_size(axis)
        shift = 1
        while shift < count:
            pairs = [(i, (i + shift) % count) for i in range(count)]
            value = jnp.maximum(value, lax.ppermute(value, axis, pairs))
            shift *= 2
    return value


def plain_body(spectral_velocity, inverse_spacing):
    planes, kx_local, width = spectral_velocity.shape[1:]
    parts = lax.axis_size("pa")
    levels = lax.axis_size("gy")
    me = lax.axis_index("pa")
    slab = NZ // parts
    plain, slope = z_table(NZ, width // 2, parts)
    order = (me - jnp.arange(parts)) % parts
    pieces = x_table(NX, KX, parts)
    pieces = np.concatenate([pieces[[-k % parts]] for k in range(2 * parts)])
    pieces = np.ascontiguousarray(np.moveaxis(pieces, 1, 0)).reshape(2, -1, NX)
    table_x = lax.dynamic_slice_in_dim(
        jnp.asarray(pieces), (parts - me) * kx_local, KX, axis=1
    ).reshape(2 * KX, NX)
    kx = (order[:, None] * kx_local + jnp.arange(kx_local)[None, :]).reshape(-1)
    wave_x = kx.astype(jnp.float32) * (2.0 * math.pi / NX)

    def exchange(modes, table):
        out = jnp.einsum(
            "dnk,fjmk->dfjnm", table, modes, precision=lax.Precision.HIGH,
            preferred_element_type=jnp.float32,
        )
        got = [lax.dynamic_index_in_dim(out, me, 0, keepdims=False)]
        for shift in range(1, parts):
            block = lax.dynamic_index_in_dim(out, (me + shift) % parts, 0, keepdims=False)
            got.append(lax.ppermute(block, "pa", [(i, (i + shift) % parts) for i in range(parts)]))
        whole = jnp.concatenate(got, axis=-1)
        return whole.reshape(whole.shape[:2] + (2, slab, KX))

    def to_x(hat):
        flat = jnp.concatenate((hat[..., 0, :, :], hat[..., 1, :, :]), axis=-1)
        return jnp.einsum(
            "...zm,mx->...zx", flat, table_x, precision=lax.Precision.HIGH,
            preferred_element_type=jnp.float32,
        )

    def turned(hat):
        return jnp.stack((-wave_x * hat[..., 1, :, :], wave_x * hat[..., 0, :, :]), axis=-3)

    u_modes, v_modes, w_modes = (spectral_velocity[c : c + 1] for c in range(3))
    uw_hat = exchange(jnp.concatenate((u_modes, w_modes)), plain)
    dzu_hat = exchange(u_modes, slope)[0]
    v_hat = exchange(v_modes, plain)[0]
    dzv_hat = exchange(v_modes, slope)[0]

    below = lax.ppermute(uw_hat[:, -1:], "gy", [(i, i + 1) for i in range(levels - 1)])
    above = lax.ppermute(uw_hat[:, :1], "gy", [(i + 1, i) for i in range(levels - 1)])
    spacing = inverse_spacing[None, :, None, None, None]
    lower = jnp.concatenate((below, uw_hat[:, :-1]), axis=1)
    upper = jnp.concatenate((uw_hat[:, 1:], above), axis=1)
    slope_y = (upper - lower) * spacing

    u, w = to_x(uw_hat[0]), to_x(uw_hat[1])
    vort_y = to_x(dzu_hat - turned(uw_hat[1]))
    v = to_x(v_hat)
    vort_z = to_x(turned(v_hat) - slope_y[0])
    vort_x = to_x(slope_y[1] - dzv_hat)
    lamb = jnp.stack(
        (v * vort_z - w * vort_y, w * vort_x - u * vort_z, u * vort_y - v * vort_x)
    )
    local_peak = jnp.max(vort_x * vort_x + vort_y * vort_y + vort_z * vort_z)
    magnitude = jnp.sqrt(everywhere_max(local_peak, ("gy", "pa")))
    return (lamb / (magnitude + 1e-06), magnitude)


def halves(table):
    table = np.asarray(table, np.float32)
    high = table.astype(ml_dtypes.bfloat16)
    low = (table - high.astype(np.float32)).astype(ml_dtypes.bfloat16)
    return high, low


def z_factors(length, modes, parts):
    slab = length // parts
    half = slab // 2
    top = modes // 2
    middle = (slab - 1) / 2
    points = np.arange(half, slab) - middle
    wave = np.arange(top + 1)
    step = 2.0 * math.pi / length
    angle = step * np.outer(points, wave)
    share = wave / top
    even = np.concatenate((np.cos(angle), -share * np.sin(angle)))
    odd = np.concatenate((np.sin(angle), share * np.cos(angle)))
    left_e, size_e, _ = np.linalg.svd(even, full_matrices=False)
    left_o, size_o, _ = np.linalg.svd(odd, full_matrices=False)
    limit = 3e-8 * max(size_e[0], size_o[0])
    rank = max(int((size_e > limit).sum()), int((size_o > limit).sum()))
    rank = min(-(-rank // 4) * 4, size_e.size, size_o.size)
    left_e, left_o = left_e[:, :rank], left_o[:, :rank]
    value = np.concatenate((
        np.concatenate((left_e[:half][::-1], left_e[:half])),
        np.concatenate((-left_o[:half][::-1], left_o[:half])),
    ), 1)
    slope = np.concatenate((
        np.concatenate((-left_e[half:][::-1], left_e[half:])),
        np.concatenate((left_o[half:][::-1], left_o[half:])),
    ), 1) * (top * step)
    column = np.arange(modes)
    signed = np.where(column < top, column, column - modes)
    kernel = np.concatenate((
        (left_e.T @ even)[:, np.abs(signed)] + 0j,
        1j * np.sign(signed) * (left_o.T @ odd)[:, np.abs(signed)],
    ))
    centre = np.arange(parts) * slab + middle
    phase = np.exp(1j * step * np.outer(centre, signed))
    return np.concatenate((value, slope)), kernel[None] * phase[:, None, :]


def z_tables(length, modes, parts):
    expand, reduce = z_factors(length, modes, parts)
    rank = expand.shape[1]
    real = np.concatenate((reduce.real, -reduce.imag), 2)
    imag = np.concatenate((reduce.imag, reduce.real), 2)
    table = np.concatenate((real, imag), 1)
    reduce = np.concatenate(halves(table), 1)
    wide = np.zeros((expand.shape[0], -(-rank // TILE) * TILE), np.float32)
    wide[:, :rank] = expand
    return reduce, np.stack(halves(wide)), rank


def x_tables(length, modes, parts):
    own = modes // parts
    column = np.arange(modes).reshape(parts, own // 2, 2).transpose(2, 0, 1)[:, :, None, :]
    step = 2.0 * math.pi / length
    angle = (column[..., None] * np.arange(length // 2) % length) * step
    weight = np.where(column == 0, 1.0, 2.0)[..., None]
    table = np.concatenate((weight * np.cos(angle), -weight * np.sin(angle)), 2)
    wave = np.concatenate((-step * column, step * column), 2).reshape(2, 1, modes)
    return (
        np.stack(halves(table.reshape(2, modes, length // 2))),
        np.tile(wave.astype(np.float32), (1, 8, 1)),
    )


def split(value):
    high = value.astype(jnp.bfloat16)
    return high, (value - high.astype(jnp.float32)).astype(jnp.bfloat16)


def dot(a, b):
    return jnp.dot(a, b, preferred_element_type=jnp.float32)


def field_kernel(
    parts, levels, rank, wave_ref, space_ref, x_hbm, reduce_hbm, expand_hbm, table_hbm,
    lamb_ref, peak_ref,
    x_ref, xt_ref, reduce_ref, expand_ref, table_ref, send, recv, halo, lhs, part_x, peaks, tile, even_ref,
    load_sem, send_sem, recv_sem, halo_send, halo_recv, peak_send, peak_recv,
):
    me, level = lax.axis_index("pa"), lax.axis_index("gy")
    planes, kx_local, width = x_ref.shape[1:]
    slab = lamb_ref.shape[2]
    two = 2 * rank
    tall = lhs.shape[0] // 4
    wide = expand_ref.shape[2]
    shifts = sorted(range(1, parts), key=lambda s: (abs(2 * s - parts), s))
    fields = (2, 0, 1)

    loads = {}

    def load(key, source, target):
        loads[key] = pltpu.make_async_copy(source, target, load_sem.at[len(loads)])
        loads[key].start()

    def slab_of(shift):
        return lax.rem(me + shift, parts)

    def rest():
        for shift in shifts[1:] + [0]:
            load(("reduce", shift), reduce_hbm.at[slab_of(shift)], reduce_ref.at[shift])
        for f in fields[1:]:
            load(("x", f), x_hbm.at[f], x_ref.at[f])
        load("table", table_hbm, table_ref)
        load("expand", expand_hbm, expand_ref)

    first = fields[0]
    load(("x", first, 0), x_hbm.at[first, 0], x_ref.at[first, 0])
    load(("reduce", shifts[0]), reduce_hbm.at[slab_of(shifts[0])], reduce_ref.at[shifts[0]])
    for j in range(1, planes):
        load(("x", first, j), x_hbm.at[first, j], x_ref.at[first, j])

    @pl.when(level == 0)
    def _():
        halo[:, 0] = jnp.zeros_like(halo[:, 0])

    @pl.when(level == levels - 1)
    def _():
        halo[:, 1] = jnp.zeros_like(halo[:, 1])

    barrier = pltpu.get_barrier_semaphore()
    others = [(a, b) for a in range(levels) for b in range(parts) if a or b]

    def other(a, b):
        return {"gy": lax.rem(level + a, levels), "pa": lax.rem(me + b, parts)}

    for a, b in others:
        pl.semaphore_signal(barrier, inc=1, device_id=other(a, b), device_id_type=MESH)

    def half(c):
        return slice(c * rank, (c + 1) * rank)

    def transfer(f, j, shift, c=None):
        rows = slice(0, two) if c is None else half(c)
        at = j + (c or 0)
        return pltpu.make_async_remote_copy(
            src_ref=send.at[f, j, shift - 1, rows],
            dst_ref=recv.at[f, j, me, rows],
            send_sem=send_sem.at[f, at, shift],
            recv_sem=recv_sem.at[f, at, shift],
            device_id={"pa": slab_of(shift)},
            device_id_type=MESH,
        )

    def arrive(f, j):
        for shift in shifts:
            transfer(f, j, shift).wait_recv()
            if f in (0, 2):
                halo_start(f, j, shift)

    def turn_modes(f, j):
        lanes = slice(j * kx_local, (j + 1) * kx_local)

        @pl.loop(0, width // 128)
        def _(n):
            at = pl.ds(pl.multiple_of(n * 128, 128), 128)
            tile[j] = x_ref[f, j, :, at]
            rows = jnp.concatenate((
                tile[j, pl.ds(0, kx_local // 2, stride=2), :],
                tile[j, pl.ds(1, kx_local // 2, stride=2), :],
            ))
            high, low = split(rows.T)
            xt_ref[0, at, lanes] = high
            xt_ref[1, at, lanes] = low

    def reduce_slab(f, shift, which):
        lanes = slice(which[0] * kx_local, (which[-1] + 1) * kx_local)
        both = dot(reduce_ref[shift], xt_ref[0, :, lanes])
        out = both[:two] + both[two:] + dot(reduce_ref[shift, :two, :], xt_ref[1, :, lanes])
        for n, j in enumerate(which):
            real = out[:rank, n * kx_local : (n + 1) * kx_local]
            imag = out[rank:, n * kx_local : (n + 1) * kx_local]
            left = lax.broadcasted_iota(jnp.int32, real.shape, 1) < kx_local // 2
            even = jnp.where(left, real, pltpu.roll(imag, kx_local // 2, 1))
            odd = jnp.where(left, pltpu.roll(real, kx_local // 2, 1), imag)
            if shift:
                send[f, j, shift - 1, half(0), :] = even
                send[f, j, shift - 1, half(1), :] = odd
            else:
                recv[f, j, me, half(0), :] = even
                recv[f, j, me, half(1), :] = odd

    def reduce_first(f):
        for j in range(planes):
            loads["x", f, j].wait()
            if j == planes - 1:
                rest()
            turn_modes(f, j)
            if j == 0:
                loads["reduce", shifts[0]].wait()
            reduce_slab(f, shifts[0], (j,))
            if j == 0:
                pl.semaphore_wait(barrier, len(others))
            transfer(f, j, shifts[0]).start()
        for shift in shifts[1:] + [0]:
            loads["reduce", shift].wait()
            reduce_slab(f, shift, range(planes))
            for j in range(planes):
                if shift:
                    transfer(f, j, shift).start()
                else:
                    halo_start(f, j, 0)

    def reduce_field(f):
        loads["x", f].wait()
        for j in range(planes):
            turn_modes(f, j)
        for shift in shifts + [0]:
            reduce_slab(f, shift, range(planes))
        if f == 0:
            for j in range(planes):
                halo_start(f, j, 0)

    def follow(f, j, before, k):
        for shift in shifts:
            transfer(before, k, shift).wait_send()
            transfer(f, j, shift).start()

    def halo_copy(f, up, shift):
        source = lax.rem(me + parts - shift, parts)
        side, j, step = (0, planes - 1, 1) if up else (1, 0, levels - 1)
        return pltpu.make_async_remote_copy(
            src_ref=recv.at[f, j, source], dst_ref=halo.at[f // 2, side, source],
            send_sem=halo_send.at[f // 2, side, shift], recv_sem=halo_recv.at[f // 2, side, shift],
            device_id={"gy": lax.rem(level + step, levels)}, device_id_type=MESH,
        )

    def halo_start(f, j, shift):
        @pl.when(level < levels - 1 if j else level > 0)
        def _():
            halo_copy(f, j > 0, shift).start()

    def halo_arrive(f):
        @pl.when(level > 0)
        def _():
            for shift in range(parts):
                halo_copy(f, True, shift).wait_recv()

        @pl.when(level < levels - 1)
        def _():
            for shift in range(parts):
                halo_copy(f, False, shift).wait_recv()

    def halo_sent(f):
        @pl.when(level < levels - 1)
        def _():
            for shift in range(parts):
                halo_copy(f, True, shift).wait_send()

        @pl.when(level > 0)
        def _():
            for shift in range(parts):
                halo_copy(f, False, shift).wait_send()

    def fill(slot, hat, classes=(0, 1)):
        @pl.loop(0, parts)
        def _(source):
            here = pl.multiple_of(source * kx_local, kx_local)
            for c in classes:
                value = hat(source, here, c)
                if tall > rank:
                    value = jnp.concatenate((value, jnp.zeros((tall - rank, kx_local), jnp.float32)))
                high, low = split(value)
                lanes = pl.ds(pl.multiple_of(c * KX + here, kx_local), kx_local)
                lhs[slot * tall : (slot + 1) * tall, lanes] = high
                lhs[(2 + slot) * tall : (3 + slot) * tall, lanes] = low

    def modes(f, j):
        return lambda source, here, c: recv[f, j, source, half(c), :]

    def turned(f, j):
        def hat(source, here, c):
            wave = wave_ref[c, 0:1, pl.ds(here, kx_local)]
            return pltpu.roll(recv[f, j, source, half(c), :], kx_local // 2, 1) * wave
        return hat

    def slope_y(f, j):
        def hat(source, here, c):
            lower = halo[f // 2, 0, source, half(c), :] if j == 0 else recv[f, j - 1, source, half(c), :]
            upper = (
                halo[f // 2, 1, source, half(c), :] if j == planes - 1
                else recv[f, j + 1, source, half(c), :]
            )
            return (upper - lower) * space_ref[j]
        return hat

    def minus(first, second):
        return lambda source, here, c: first(source, here, c) - second(source, here, c)

    def of_class(c, at):
        lanes = slice(c * KX, (c + 1) * KX)
        both = dot(lhs[:, lanes], table_ref[0, c, :, at])
        return both[: 2 * tall] + both[2 * tall :] + dot(lhs[: 2 * tall, lanes], table_ref[1, c, :, at])

    def to_x(at, even=None):
        even = of_class(0, at) if even is None else even
        odd = of_class(1, at)
        out = jnp.concatenate((even + odd, even - odd), 1)
        return out[:tall], out[tall:]

    def to_z(value, rows):
        if wide > tall:
            value = jnp.concatenate((value, jnp.zeros((wide - tall, 2 * TILE), jnp.float32)))
        high, low = split(value)
        return (
            dot(expand_ref[0, :rows, :], high)
            + dot(expand_ref[1, :rows, :], high)
            + dot(expand_ref[0, :rows, :], low)
        )

    def tiles(step, init, unroll=False):
        def at_tile(t, carry):
            at = pl.ds(pl.multiple_of(t * TILE, TILE), TILE)
            far = pl.ds(pl.multiple_of(NX // 2 + t * TILE, TILE), TILE)
            return step(at, ((slice(0, TILE), at), (slice(TILE, 2 * TILE), far)), carry)
        return lax.fori_loop(0, NX // 2 // TILE, at_tile, init, unroll=unroll)

    reduce_first(first)
    for f in fields[1:]:
        reduce_field(f)
    loads["table"].wait()
    loads["expand"].wait()

    for j in range(planes):
        follow(0, j, 2, j)
    for j in range(planes):
        arrive(2, j)
    for j in range(planes):
        fill(0, modes(2, j))
        fill(1, turned(2, j))

        def w_tile(at, sides, carry):
            w, dx_w = to_x(at)
            w, dx_w = to_z(w, slab), to_z(dx_w, slab)
            for part, to in sides:
                lamb_ref[1, j, :, to] = w[:, part]
                lamb_ref[2, j, :, to] = dx_w[:, part]
            return carry

        tiles(w_tile, 0)

    arrive(0, 0)
    halo_arrive(2)
    for j in range(planes):
        fill(j, slope_y(2, j))

    def dy_tile(at, sides, carry):
        for j, value in enumerate(to_x(at)):
            value = to_z(value, slab)
            for part, to in sides:
                part_x[j, :, to] = value[:, part]
        return carry

    tiles(dy_tile, 0)

    follow(1, 0, 0, 1)
    last = planes - 1
    for shift in shifts:
        transfer(0, 0, shift).wait_send()
        transfer(1, last, shift, 0).start()
    for shift in shifts:
        transfer(1, last, shift, 1).start()
    arrive(0, 1)
    for j in range(planes):
        fill(j, modes(0, j))

    def u_tile(at, sides, carry):
        for j, value in enumerate(to_x(at)):
            both = to_z(value, 2 * slab)
            for part, to in sides:
                lamb_ref[0, j, :, to] = both[:slab, part]
                lamb_ref[2, j, :, to] = both[slab:, part] - lamb_ref[2, j, :, to]
        return carry

    tiles(u_tile, 0)
    halo_arrive(0)

    top = jnp.zeros((8, TILE), jnp.float32)
    for j in range(planes):
        hats = modes(1, j), minus(turned(1, j), slope_y(0, j))
        if j < last:
            arrive(1, j)
            for slot in range(2):
                fill(slot, hats[slot])
        else:
            for c in range(2):
                for shift in shifts:
                    transfer(1, last, shift, c).wait_recv()
                for slot in range(2):
                    fill(slot, hats[slot], (c,))
                if c == 0:
                    def even_tile(at, sides, carry):
                        even_ref[:, at] = of_class(0, at)
                        return carry

                    tiles(even_tile, 0)

        def v_tile(at, sides, top):
            value, turn = to_x(at, even_ref[:, at] if j == last else None)
            value = to_z(value, 2 * slab)
            turn = to_z(turn, slab)
            for part, to in sides:
                v, vort_z = value[:slab, part], turn[:, part]
                vort_x = part_x[j, :, to] - value[slab:, part]
                u, w, vort_y = lamb_ref[0, j, :, to], lamb_ref[1, j, :, to], lamb_ref[2, j, :, to]
                lamb_ref[0, j, :, to] = v * vort_z - w * vort_y
                lamb_ref[1, j, :, to] = w * vort_x - u * vort_z
                lamb_ref[2, j, :, to] = u * vort_y - v * vort_x
                square = vort_x * vort_x + vort_y * vort_y + vort_z * vort_z
                top = jnp.maximum(top, square.reshape(slab // 8, 8, TILE).max(0))
            return top

        top = tiles(v_tile, top, j == last)

    value = top[:, :128]
    for k in range(1, TILE // 128):
        value = jnp.maximum(value, top[:, k * 128 : (k + 1) * 128])
    peaks[0] = value.max(0, keepdims=True)
    copies = [
        pltpu.make_async_remote_copy(
            src_ref=peaks.at[0], dst_ref=peaks.at[n + 1],
            send_sem=peak_send.at[n], recv_sem=peak_recv.at[n],
            device_id=other(a, b), device_id_type=MESH,
        )
        for n, (a, b) in enumerate(others)
    ]
    for copy in copies:
        copy.start()
    for copy in copies:
        copy.wait_recv()
    value = peaks[...].max(0)
    peak = jnp.sqrt(jnp.max(value, axis=(0, 1), keepdims=True))
    peak_ref[...] = jnp.broadcast_to(peak, peak_ref.shape)

    for shift in shifts:
        for j in range(last):
            transfer(1, j, shift).wait_send()
        for c in range(2):
            transfer(1, last, shift, c).wait_send()
    halo_sent(0)
    halo_sent(2)
    for copy in copies:
        copy.wait_send()


def scale_kernel(lamb_ref, peak_ref, out_hbm, top_ref, held, sem):
    top_ref[...] = peak_ref[0:1, 0:1]
    scale = 1.0 / (peak_ref[0:1, 0:1] + 1e-06)
    slots, rows, _ = held.shape
    per = lamb_ref.shape[2] // rows
    places = [
        (c, j, k) for c in range(lamb_ref.shape[0]) for j in range(lamb_ref.shape[1]) for k in range(per)
    ]
    copies = []
    for n, (c, j, k) in enumerate(places):
        at = pl.ds(k * rows, rows)
        if n >= slots:
            copies[n - slots].wait()

        @pl.loop(0, rows // 16)
        def _(i):
            part = pl.ds(pl.multiple_of(i * 16, 16), 16)
            held[n % slots, part, :] = lamb_ref[c, j, pl.ds(pl.multiple_of(k * rows + i * 16, 16), 16), :] * scale

        copies.append(pltpu.make_async_copy(
            held.at[n % slots], out_hbm.at[c, j, at], sem.at[n % slots]
        ))
        copies[n].start()
    for copy in copies[-slots:]:
        copy.wait()


def body(spectral_velocity, inverse_spacing):
    planes, kx_local, width = spectral_velocity.shape[1:]
    parts, levels = lax.axis_size("pa"), lax.axis_size("gy")
    slab = NZ // parts
    if planes != 2 or kx_local % 128 or slab % 16 or parts < 2 or levels < 2:
        return plain_body(spectral_velocity, inverse_spacing)
    reduce, expand, rank = z_tables(NZ, width // 2, parts)
    table, wave = x_tables(NX, KX, parts)
    tall = -(-rank // 16) * 16
    hbm = pl.BlockSpec(memory_space=pl.ANY)
    vmem = pl.BlockSpec(memory_space=pltpu.VMEM)
    block = (parts, 2 * rank, kx_local)
    dma = pltpu.SemaphoreType.DMA
    lamb, peak = pl.pallas_call(
        functools.partial(field_kernel, parts, levels, rank),
        out_shape=(
            pltpu.VMEM((3, planes, slab, NX), jnp.float32),
            pltpu.VMEM((8, 128), jnp.float32),
        ),
        in_specs=[vmem, pl.BlockSpec(memory_space=pltpu.SMEM), hbm, hbm, hbm, hbm],
        out_specs=(vmem, vmem),
        scratch_shapes=[
            pltpu.VMEM((3, planes, kx_local, width), jnp.float32),
            pltpu.VMEM((2, width, planes * kx_local), jnp.bfloat16),
            pltpu.VMEM(reduce.shape, jnp.bfloat16),
            pltpu.VMEM(expand.shape, jnp.bfloat16),
            pltpu.VMEM(table.shape, jnp.bfloat16),
            pltpu.VMEM((3, planes, parts - 1) + block[1:], jnp.float32),
            pltpu.VMEM((3, planes) + block, jnp.float32),
            pltpu.VMEM((2, 2) + block, jnp.float32),
            pltpu.VMEM((4 * tall, 2 * KX), jnp.bfloat16),
            pltpu.VMEM((planes, slab, NX), jnp.float32),
            pltpu.VMEM((parts * levels, 1, 128), jnp.float32),
            pltpu.VMEM((planes, kx_local, 128), jnp.float32),
            pltpu.VMEM((2 * tall, NX // 2), jnp.float32),
            dma((parts + 6,)),
            dma((3, planes + 1, parts)),
            dma((3, planes + 1, parts)),
            dma((2, 2, parts)),
            dma((2, 2, parts)),
            dma((parts * levels - 1,)),
            dma((parts * levels - 1,)),
        ],
        compiler_params=pltpu.CompilerParams(
            collective_id=0, has_side_effects=True, vmem_limit_bytes=51 * 2**20
        ),
    )(wave, inverse_spacing, spectral_velocity, reduce, expand, table)
    out, top = pl.pallas_call(
        scale_kernel,
        out_shape=(
            jax.ShapeDtypeStruct(lamb.shape, jnp.float32),
            jax.ShapeDtypeStruct((1, 1), jnp.float32),
        ),
        in_specs=[vmem, vmem],
        out_specs=(hbm, vmem),
        scratch_shapes=[pltpu.VMEM((8, slab // 6, NX), jnp.float32), dma((8,))],
        compiler_params=pltpu.CompilerParams(vmem_limit_bytes=6 * 2**20),
    )(
        pltpu.with_memory_space_constraint(lamb, pltpu.VMEM),
        pltpu.with_memory_space_constraint(peak, pltpu.VMEM),
    )
    return out, top[0, 0]


def solution(mesh):
    placed = (P(None, "gy", "pa", None), P("gy"))
    return jax.shard_map(
        body,
        mesh=mesh,
        in_specs=placed,
        out_specs=(P(None, "gy", "pa", None), P()),
        check_vma=False,
    )
```

```python
import functools
import math

import ml_dtypes
import numpy as np

import jax
import jax.numpy as jnp
from jax import lax
from jax.experimental import pallas as pl
from jax.experimental.pallas import tpu as pltpu
from jax.sharding import PartitionSpec as P

NX = 1536
NZ = 1152
KX = 512
MESH = pl.DeviceIdType.MESH
TILE = 256


def z_table(length, modes, parts):
    column = np.arange(modes)
    wave = np.where(column < modes // 2, column, column - modes)
    angles = (wave[None, :] * np.arange(length)[:, None] % length) * (2.0 * math.pi / length)
    cos, sin = np.cos(angles), np.sin(angles)
    scale = (wave * (2.0 * math.pi / length))[None, :]

    def lay(rr, ri, ir, ii):
        real = np.concatenate((rr, ri), 1).reshape(parts, 1, length // parts, 2 * modes)
        imag = np.concatenate((ir, ii), 1).reshape(parts, 1, length // parts, 2 * modes)
        both = np.concatenate((real, imag), 1)
        return both.reshape(parts, -1, 2 * modes).astype(np.float32)

    plain = lay(cos, -sin, sin, cos)
    slope = lay(-scale * sin, -scale * cos, scale * cos, -scale * sin)
    return plain, slope


def x_table(length, modes, parts):
    column = np.arange(modes)
    angles = (column[:, None] * np.arange(length)[None, :] % length) * (2.0 * math.pi / length)
    weight = np.where(column == 0, 1.0, 2.0)[:, None]
    both = np.stack((weight * np.cos(angles), -weight * np.sin(angles)))
    both = both.reshape(2, parts, modes // parts, length)
    return np.moveaxis(both, 1, 0).astype(np.float32)


def everywhere_max(value, axes):
    for axis in axes:
        count = lax.axis_size(axis)
        shift = 1
        while shift < count:
            pairs = [(i, (i + shift) % count) for i in range(count)]
            value = jnp.maximum(value, lax.ppermute(value, axis, pairs))
            shift *= 2
    return value


def plain_body(spectral_velocity, inverse_spacing):
    planes, kx_local, width = spectral_velocity.shape[1:]
    parts = lax.axis_size("pa")
    levels = lax.axis_size("gy")
    me = lax.axis_index("pa")
    slab = NZ // parts
    plain, slope = z_table(NZ, width // 2, parts)
    order = (me - jnp.arange(parts)) % parts
    pieces = x_table(NX, KX, parts)
    pieces = np.concatenate([pieces[[-k % parts]] for k in range(2 * parts)])
    pieces = np.ascontiguousarray(np.moveaxis(pieces, 1, 0)).reshape(2, -1, NX)
    table_x = lax.dynamic_slice_in_dim(
        jnp.asarray(pieces), (parts - me) * kx_local, KX, axis=1
    ).reshape(2 * KX, NX)
    kx = (order[:, None] * kx_local + jnp.arange(kx_local)[None, :]).reshape(-1)
    wave_x = kx.astype(jnp.float32) * (2.0 * math.pi / NX)

    def exchange(modes, table):
        out = jnp.einsum(
            "dnk,fjmk->dfjnm", table, modes, precision=lax.Precision.HIGH,
            preferred_element_type=jnp.float32,
        )
        got = [lax.dynamic_index_in_dim(out, me, 0, keepdims=False)]
        for shift in range(1, parts):
            block = lax.dynamic_index_in_dim(out, (me + shift) % parts, 0, keepdims=False)
            got.append(lax.ppermute(block, "pa", [(i, (i + shift) % parts) for i in range(parts)]))
        whole = jnp.concatenate(got, axis=-1)
        return whole.reshape(whole.shape[:2] + (2, slab, KX))

    def to_x(hat):
        flat = jnp.concatenate((hat[..., 0, :, :], hat[..., 1, :, :]), axis=-1)
        return jnp.einsum(
            "...zm,mx->...zx", flat, table_x, precision=lax.Precision.HIGH,
            preferred_element_type=jnp.float32,
        )

    def turned(hat):
        return jnp.stack((-wave_x * hat[..., 1, :, :], wave_x * hat[..., 0, :, :]), axis=-3)

    u_modes, v_modes, w_modes = (spectral_velocity[c : c + 1] for c in range(3))
    uw_hat = exchange(jnp.concatenate((u_modes, w_modes)), plain)
    dzu_hat = exchange(u_modes, slope)[0]
    v_hat = exchange(v_modes, plain)[0]
    dzv_hat = exchange(v_modes, slope)[0]

    below = lax.ppermute(uw_hat[:, -1:], "gy", [(i, i + 1) for i in range(levels - 1)])
    above = lax.ppermute(uw_hat[:, :1], "gy", [(i + 1, i) for i in range(levels - 1)])
    spacing = inverse_spacing[None, :, None, None, None]
    lower = jnp.concatenate((below, uw_hat[:, :-1]), axis=1)
    upper = jnp.concatenate((uw_hat[:, 1:], above), axis=1)
    slope_y = (upper - lower) * spacing

    u, w = to_x(uw_hat[0]), to_x(uw_hat[1])
    vort_y = to_x(dzu_hat - turned(uw_hat[1]))
    v = to_x(v_hat)
    vort_z = to_x(turned(v_hat) - slope_y[0])
    vort_x = to_x(slope_y[1] - dzv_hat)
    lamb = jnp.stack(
        (v * vort_z - w * vort_y, w * vort_x - u * vort_z, u * vort_y - v * vort_x)
    )
    local_peak = jnp.max(vort_x * vort_x + vort_y * vort_y + vort_z * vort_z)
    magnitude = jnp.sqrt(everywhere_max(local_peak, ("gy", "pa")))
    return (lamb / (magnitude + 1e-06), magnitude)


def halves(table):
    table = np.asarray(table, np.float32)
    high = table.astype(ml_dtypes.bfloat16)
    low = (table - high.astype(np.float32)).astype(ml_dtypes.bfloat16)
    return high, low


def z_factors(length, modes, parts):
    slab = length // parts
    half = slab // 2
    top = modes // 2
    middle = (slab - 1) / 2
    points = np.arange(half, slab) - middle
    wave = np.arange(top + 1)
    step = 2.0 * math.pi / length
    angle = step * np.outer(points, wave)
    share = wave / top
    even = np.concatenate((np.cos(angle), -share * np.sin(angle)))
    odd = np.concatenate((np.sin(angle), share * np.cos(angle)))
    left_e, size_e, _ = np.linalg.svd(even, full_matrices=False)
    left_o, size_o, _ = np.linalg.svd(odd, full_matrices=False)
    limit = 3e-8 * max(size_e[0], size_o[0])
    rank = max(int((size_e > limit).sum()), int((size_o > limit).sum()))
    rank = min(-(-rank // 4) * 4, size_e.size, size_o.size)
    left_e, left_o = left_e[:, :rank], left_o[:, :rank]
    value = np.concatenate((
        np.concatenate((left_e[:half][::-1], left_e[:half])),
        np.concatenate((-left_o[:half][::-1], left_o[:half])),
    ), 1)
    slope = np.concatenate((
        np.concatenate((-left_e[half:][::-1], left_e[half:])),
        np.concatenate((left_o[half:][::-1], left_o[half:])),
    ), 1) * (top * step)
    column = np.arange(modes)
    signed = np.where(column < top, column, column - modes)
    kernel = np.concatenate((
        (left_e.T @ even)[:, np.abs(signed)] + 0j,
        1j * np.sign(signed) * (left_o.T @ odd)[:, np.abs(signed)],
    ))
    centre = np.arange(parts) * slab + middle
    phase = np.exp(1j * step * np.outer(centre, signed))
    return np.concatenate((value, slope)), kernel[None] * phase[:, None, :]


def z_tables(length, modes, parts):
    expand, reduce = z_factors(length, modes, parts)
    rank = expand.shape[1]
    real = np.concatenate((reduce.real, -reduce.imag), 2)
    imag = np.concatenate((reduce.imag, reduce.real), 2)
    table = np.concatenate((real, imag), 1)
    reduce = np.concatenate(halves(table), 1)
    wide = np.zeros((expand.shape[0], -(-rank // TILE) * TILE), np.float32)
    wide[:, :rank] = expand
    return reduce, np.stack(halves(wide)), rank


def x_tables(length, modes, parts):
    own = modes // parts
    column = np.arange(modes).reshape(parts, own // 2, 2).transpose(2, 0, 1)[:, :, None, :]
    step = 2.0 * math.pi / length
    angle = (column[..., None] * np.arange(length // 2) % length) * step
    weight = np.where(column == 0, 1.0, 2.0)[..., None]
    table = np.concatenate((weight * np.cos(angle), -weight * np.sin(angle)), 2)
    wave = np.concatenate((-step * column, step * column), 2).reshape(2, 1, modes)
    return (
        np.stack(halves(table.reshape(2, modes, length // 2))),
        np.tile(wave.astype(np.float32), (1, 8, 1)),
    )


def split(value):
    high = value.astype(jnp.bfloat16)
    return high, (value - high.astype(jnp.float32)).astype(jnp.bfloat16)


def dot(a, b):
    return jnp.dot(a, b, preferred_element_type=jnp.float32)


def field_kernel(
    parts, levels, rank, wave_hbm, space_ref, x_hbm, reduce_hbm, expand_hbm, table_hbm,
    lamb_ref, peak_ref,
    x_ref, xt_ref, reduce_ref, expand_ref, table_ref, send, recv, halo, lhs, part_x, peaks, tile, even_ref, wave_ref,
    load_sem, send_sem, recv_sem, halo_send, halo_recv, peak_send, peak_recv,
):
    me, level = lax.axis_index("pa"), lax.axis_index("gy")
    planes, kx_local, width = x_ref.shape[1:]
    slab = lamb_ref.shape[2]
    two = 2 * rank
    tall = lhs.shape[0] // 4
    wide = expand_ref.shape[2]
    shifts = sorted(range(1, parts), key=lambda s: (abs(2 * s - parts), s))
    fields = (2, 0, 1)

    loads = {}

    def load(key, source, target):
        loads[key] = pltpu.make_async_copy(source, target, load_sem.at[len(loads)])
        loads[key].start()

    def slab_of(shift):
        return lax.rem(me + shift, parts)

    def rest():
        for shift in shifts[1:] + [0]:
            load(("reduce", shift), reduce_hbm.at[slab_of(shift)], reduce_ref.at[shift])
        for f in fields[1:]:
            load(("x", f), x_hbm.at[f], x_ref.at[f])
        load("table", table_hbm, table_ref)
        load("expand", expand_hbm, expand_ref)
        load("wave", wave_hbm, wave_ref)

    first = fields[0]
    load(("x", first, 0), x_hbm.at[first, 0], x_ref.at[first, 0])
    load(("reduce", shifts[0]), reduce_hbm.at[slab_of(shifts[0])], reduce_ref.at[shifts[0]])
    for j in range(1, planes):
        load(("x", first, j), x_hbm.at[first, j], x_ref.at[first, j])

    @pl.when(level == 0)
    def _():
        halo[:, 0] = jnp.zeros_like(halo[:, 0])

    @pl.when(level == levels - 1)
    def _():
        halo[:, 1] = jnp.zeros_like(halo[:, 1])

    barrier = pltpu.get_barrier_semaphore()
    others = [(a, b) for a in range(levels) for b in range(parts) if a or b]

    def other(a, b):
        return {"gy": lax.rem(level + a, levels), "pa": lax.rem(me + b, parts)}

    for a, b in others:
        pl.semaphore_signal(barrier, inc=1, device_id=other(a, b), device_id_type=MESH)

    def half(c):
        return slice(c * rank, (c + 1) * rank)

    def transfer(f, j, shift, c=None):
        rows = slice(0, two) if c is None else half(c)
        at = j + (c or 0)
        return pltpu.make_async_remote_copy(
            src_ref=send.at[f, j, shift - 1, rows],
            dst_ref=recv.at[f, j, me, rows],
            send_sem=send_sem.at[f, at, shift],
            recv_sem=recv_sem.at[f, at, shift],
            device_id={"pa": slab_of(shift)},
            device_id_type=MESH,
        )

    def arrive(f, j):
        for shift in shifts:
            transfer(f, j, shift).wait_recv()
            if f in (0, 2):
                halo_start(f, j, shift)

    def turn_modes(f, j):
        lanes = slice(j * kx_local, (j + 1) * kx_local)

        for n in range(width // 128):
            at = slice(n * 128, (n + 1) * 128)
            tile[n] = x_ref[f, j, :, at]
            rows = jnp.concatenate((
                tile[n, pl.ds(0, kx_local // 2, stride=2), :],
                tile[n, pl.ds(1, kx_local // 2, stride=2), :],
            ))
            high, low = split(rows.T)
            xt_ref[0, at, lanes] = high
            xt_ref[1, at, lanes] = low

    def reduce_slab(f, shift, which):
        lanes = slice(which[0] * kx_local, (which[-1] + 1) * kx_local)
        both = dot(reduce_ref[shift], xt_ref[0, :, lanes])
        out = both[:two] + both[two:] + dot(reduce_ref[shift, :two, :], xt_ref[1, :, lanes])
        for n, j in enumerate(which):
            real = out[:rank, n * kx_local : (n + 1) * kx_local]
            imag = out[rank:, n * kx_local : (n + 1) * kx_local]
            left = lax.broadcasted_iota(jnp.int32, real.shape, 1) < kx_local // 2
            even = jnp.where(left, real, pltpu.roll(imag, kx_local // 2, 1))
            odd = jnp.where(left, pltpu.roll(real, kx_local // 2, 1), imag)
            if shift:
                send[f, j, shift - 1, half(0), :] = even
                send[f, j, shift - 1, half(1), :] = odd
            else:
                recv[f, j, me, half(0), :] = even
                recv[f, j, me, half(1), :] = odd

    def reduce_first(f):
        for j in range(planes):
            loads["x", f, j].wait()
            if j == planes - 1:
                rest()
            turn_modes(f, j)
            if j == 0:
                loads["reduce", shifts[0]].wait()
            reduce_slab(f, shifts[0], (j,))
            if j == 0:
                pl.semaphore_wait(barrier, len(others))
            transfer(f, j, shifts[0]).start()
        for shift in shifts[1:] + [0]:
            loads["reduce", shift].wait()
            reduce_slab(f, shift, range(planes))
            for j in range(planes):
                if shift:
                    transfer(f, j, shift).start()
                else:
                    halo_start(f, j, 0)

    def reduce_field(f):
        loads["x", f].wait()
        for j in range(planes):
            turn_modes(f, j)
        for shift in shifts + [0]:
            reduce_slab(f, shift, range(planes))
        if f == 0:
            for j in range(planes):
                halo_start(f, j, 0)

    def follow(f, j, before, k):
        for shift in shifts:
            transfer(before, k, shift).wait_send()
            transfer(f, j, shift).start()

    def halo_copy(f, up, shift):
        source = lax.rem(me + parts - shift, parts)
        side, j, step = (0, planes - 1, 1) if up else (1, 0, levels - 1)
        return pltpu.make_async_remote_copy(
            src_ref=recv.at[f, j, source], dst_ref=halo.at[f // 2, side, source],
            send_sem=halo_send.at[f // 2, side, shift], recv_sem=halo_recv.at[f // 2, side, shift],
            device_id={"gy": lax.rem(level + step, levels)}, device_id_type=MESH,
        )

    def halo_start(f, j, shift):
        @pl.when(level < levels - 1 if j else level > 0)
        def _():
            halo_copy(f, j > 0, shift).start()

    def halo_arrive(f):
        @pl.when(level > 0)
        def _():
            for shift in range(parts):
                halo_copy(f, True, shift).wait_recv()

        @pl.when(level < levels - 1)
        def _():
            for shift in range(parts):
                halo_copy(f, False, shift).wait_recv()

    def halo_sent(f):
        @pl.when(level < levels - 1)
        def _():
            for shift in range(parts):
                halo_copy(f, True, shift).wait_send()

        @pl.when(level > 0)
        def _():
            for shift in range(parts):
                halo_copy(f, False, shift).wait_send()

    def fill(slot, hat, classes=(0, 1)):
        @pl.loop(0, parts)
        def _(source):
            here = pl.multiple_of(source * kx_local, kx_local)
            for c in classes:
                value = hat(source, here, c)
                if tall > rank:
                    value = jnp.concatenate((value, jnp.zeros((tall - rank, kx_local), jnp.float32)))
                high, low = split(value)
                lanes = pl.ds(pl.multiple_of(c * KX + here, kx_local), kx_local)
                lhs[slot * tall : (slot + 1) * tall, lanes] = high
                lhs[(2 + slot) * tall : (3 + slot) * tall, lanes] = low

    def modes(f, j):
        return lambda source, here, c: recv[f, j, source, half(c), :]

    def turned(f, j):
        def hat(source, here, c):
            wave = wave_ref[c, 0:1, pl.ds(here, kx_local)]
            return pltpu.roll(recv[f, j, source, half(c), :], kx_local // 2, 1) * wave
        return hat

    def slope_y(f, j):
        def hat(source, here, c):
            lower = halo[f // 2, 0, source, half(c), :] if j == 0 else recv[f, j - 1, source, half(c), :]
            upper = (
                halo[f // 2, 1, source, half(c), :] if j == planes - 1
                else recv[f, j + 1, source, half(c), :]
            )
            return (upper - lower) * space_ref[j]
        return hat

    def minus(first, second):
        return lambda source, here, c: first(source, here, c) - second(source, here, c)

    def of_class(c, at):
        lanes = slice(c * KX, (c + 1) * KX)
        both = dot(lhs[:, lanes], table_ref[0, c, :, at])
        return both[: 2 * tall] + both[2 * tall :] + dot(lhs[: 2 * tall, lanes], table_ref[1, c, :, at])

    def to_x(at, even=None):
        even = of_class(0, at) if even is None else even
        odd = of_class(1, at)
        out = jnp.concatenate((even + odd, even - odd), 1)
        return out[:tall], out[tall:]

    def to_z(value, rows):
        if wide > tall:
            value = jnp.concatenate((value, jnp.zeros((wide - tall, 2 * TILE), jnp.float32)))
        high, low = split(value)
        return (
            dot(expand_ref[0, :rows, :], high)
            + dot(expand_ref[1, :rows, :], high)
            + dot(expand_ref[0, :rows, :], low)
        )

    def tiles(step, init, unroll=False):
        def at_tile(t, carry):
            at = pl.ds(pl.multiple_of(t * TILE, TILE), TILE)
            far = pl.ds(pl.multiple_of(NX // 2 + t * TILE, TILE), TILE)
            return step(at, ((slice(0, TILE), at), (slice(TILE, 2 * TILE), far)), carry)
        return lax.fori_loop(0, NX // 2 // TILE, at_tile, init, unroll=unroll)

    reduce_first(first)
    for f in fields[1:]:
        reduce_field(f)
    loads["table"].wait()
    loads["expand"].wait()
    loads["wave"].wait()

    for j in range(planes):
        follow(0, j, 2, j)
    for j in range(planes):
        arrive(2, j)
    for j in range(planes):
        fill(0, modes(2, j))
        fill(1, turned(2, j))

        def w_tile(at, sides, carry):
            w, dx_w = to_x(at)
            w, dx_w = to_z(w, slab), to_z(dx_w, slab)
            for part, to in sides:
                lamb_ref[1, j, :, to] = w[:, part]
                lamb_ref[2, j, :, to] = dx_w[:, part]
            return carry

        tiles(w_tile, 0)

    arrive(0, 0)
    halo_arrive(2)
    for j in range(planes):
        fill(j, slope_y(2, j))

    def dy_tile(at, sides, carry):
        for j, value in enumerate(to_x(at)):
            value = to_z(value, slab)
            for part, to in sides:
                part_x[j, :, to] = value[:, part]
        return carry

    tiles(dy_tile, 0)

    follow(1, 0, 0, 1)
    last = planes - 1
    for shift in shifts:
        transfer(0, 0, shift).wait_send()
        transfer(1, last, shift, 0).start()
    for shift in shifts:
        transfer(1, last, shift, 1).start()
    arrive(0, 1)
    for j in range(planes):
        fill(j, modes(0, j))

    def u_tile(at, sides, carry):
        for j, value in enumerate(to_x(at)):
            both = to_z(value, 2 * slab)
            for part, to in sides:
                lamb_ref[0, j, :, to] = both[:slab, part]
                lamb_ref[2, j, :, to] = both[slab:, part] - lamb_ref[2, j, :, to]
        return carry

    tiles(u_tile, 0)
    halo_arrive(0)

    top = jnp.zeros((8, TILE), jnp.float32)
    for j in range(planes):
        hats = modes(1, j), minus(turned(1, j), slope_y(0, j))
        if j < last:
            arrive(1, j)
            for slot in range(2):
                fill(slot, hats[slot])
        else:
            for c in range(2):
                for shift in shifts:
                    transfer(1, last, shift, c).wait_recv()
                for slot in range(2):
                    fill(slot, hats[slot], (c,))
                if c == 0:
                    def even_tile(at, sides, carry):
                        even_ref[:, at] = of_class(0, at)
                        return carry

                    tiles(even_tile, 0)

        def v_tile(at, sides, top):
            value, turn = to_x(at, even_ref[:, at] if j == last else None)
            value = to_z(value, 2 * slab)
            turn = to_z(turn, slab)
            for part, to in sides:
                v, vort_z = value[:slab, part], turn[:, part]
                vort_x = part_x[j, :, to] - value[slab:, part]
                u, w, vort_y = lamb_ref[0, j, :, to], lamb_ref[1, j, :, to], lamb_ref[2, j, :, to]
                lamb_ref[0, j, :, to] = v * vort_z - w * vort_y
                lamb_ref[1, j, :, to] = w * vort_x - u * vort_z
                lamb_ref[2, j, :, to] = u * vort_y - v * vort_x
                square = vort_x * vort_x + vort_y * vort_y + vort_z * vort_z
                top = jnp.maximum(top, square.reshape(slab // 8, 8, TILE).max(0))
            return top

        top = tiles(v_tile, top, j == last)

    value = top[:, :128]
    for k in range(1, TILE // 128):
        value = jnp.maximum(value, top[:, k * 128 : (k + 1) * 128])
    peaks[0] = value.max(0, keepdims=True)
    copies = [
        pltpu.make_async_remote_copy(
            src_ref=peaks.at[0], dst_ref=peaks.at[n + 1],
            send_sem=peak_send.at[n], recv_sem=peak_recv.at[n],
            device_id=other(a, b), device_id_type=MESH,
        )
        for n, (a, b) in enumerate(others)
    ]
    for copy in copies:
        copy.start()
    for copy in copies:
        copy.wait_recv()
    value = peaks[...].max(0)
    peak = jnp.sqrt(jnp.max(value, axis=(0, 1), keepdims=True))
    peak_ref[...] = jnp.broadcast_to(peak, peak_ref.shape)

    for shift in shifts:
        for j in range(last):
            transfer(1, j, shift).wait_send()
        for c in range(2):
            transfer(1, last, shift, c).wait_send()
    halo_sent(0)
    halo_sent(2)
    for copy in copies:
        copy.wait_send()


def scale_kernel(lamb_ref, peak_ref, out_hbm, top_ref, held, sem):
    top_ref[...] = peak_ref[0:1, 0:1]
    scale = 1.0 / (peak_ref[0:1, 0:1] + 1e-06)
    slots, rows, _ = held.shape
    per = lamb_ref.shape[2] // rows
    places = [
        (c, j, k) for c in range(lamb_ref.shape[0]) for j in range(lamb_ref.shape[1]) for k in range(per)
    ]
    copies = []
    for n, (c, j, k) in enumerate(places):
        at = pl.ds(k * rows, rows)
        if n >= slots:
            copies[n - slots].wait()

        @pl.loop(0, rows // 16)
        def _(i):
            part = pl.ds(pl.multiple_of(i * 16, 16), 16)
            held[n % slots, part, :] = lamb_ref[c, j, pl.ds(pl.multiple_of(k * rows + i * 16, 16), 16), :] * scale

        copies.append(pltpu.make_async_copy(
            held.at[n % slots], out_hbm.at[c, j, at], sem.at[n % slots]
        ))
        copies[n].start()
    for copy in copies[-slots:]:
        copy.wait()


def body(spectral_velocity, inverse_spacing):
    planes, kx_local, width = spectral_velocity.shape[1:]
    parts, levels = lax.axis_size("pa"), lax.axis_size("gy")
    slab = NZ // parts
    if planes != 2 or kx_local % 128 or slab % 16 or parts < 2 or levels < 2:
        return plain_body(spectral_velocity, inverse_spacing)
    reduce, expand, rank = z_tables(NZ, width // 2, parts)
    table, wave = x_tables(NX, KX, parts)
    tall = -(-rank // 16) * 16
    hbm = pl.BlockSpec(memory_space=pl.ANY)
    vmem = pl.BlockSpec(memory_space=pltpu.VMEM)
    block = (parts, 2 * rank, kx_local)
    dma = pltpu.SemaphoreType.DMA
    lamb, peak = pl.pallas_call(
        functools.partial(field_kernel, parts, levels, rank),
        out_shape=(
            pltpu.VMEM((3, planes, slab, NX), jnp.float32),
            pltpu.VMEM((8, 128), jnp.float32),
        ),
        in_specs=[hbm, pl.BlockSpec(memory_space=pltpu.SMEM), hbm, hbm, hbm, hbm],
        out_specs=(vmem, vmem),
        scratch_shapes=[
            pltpu.VMEM((3, planes, kx_local, width), jnp.float32),
            pltpu.VMEM((2, width, planes * kx_local), jnp.bfloat16),
            pltpu.VMEM(reduce.shape, jnp.bfloat16),
            pltpu.VMEM(expand.shape, jnp.bfloat16),
            pltpu.VMEM(table.shape, jnp.bfloat16),
            pltpu.VMEM((3, planes, parts - 1) + block[1:], jnp.float32),
            pltpu.VMEM((3, planes) + block, jnp.float32),
            pltpu.VMEM((2, 2) + block, jnp.float32),
            pltpu.VMEM((4 * tall, 2 * KX), jnp.bfloat16),
            pltpu.VMEM((planes, slab, NX), jnp.float32),
            pltpu.VMEM((parts * levels, 1, 128), jnp.float32),
            pltpu.VMEM((width // 128, kx_local, 128), jnp.float32),
            pltpu.VMEM((2 * tall, NX // 2), jnp.float32),
            pltpu.VMEM(wave.shape, jnp.float32),
            dma((parts + 7,)),
            dma((3, planes + 1, parts)),
            dma((3, planes + 1, parts)),
            dma((2, 2, parts)),
            dma((2, 2, parts)),
            dma((parts * levels - 1,)),
            dma((parts * levels - 1,)),
        ],
        compiler_params=pltpu.CompilerParams(
            collective_id=0, has_side_effects=True, vmem_limit_bytes=51 * 2**20
        ),
    )(wave, inverse_spacing, spectral_velocity, reduce, expand, table)
    out, top = pl.pallas_call(
        scale_kernel,
        out_shape=(
            jax.ShapeDtypeStruct(lamb.shape, jnp.float32),
            jax.ShapeDtypeStruct((1, 1), jnp.float32),
        ),
        in_specs=[vmem, vmem],
        out_specs=(hbm, vmem),
        scratch_shapes=[pltpu.VMEM((8, slab // 6, NX), jnp.float32), dma((8,))],
        compiler_params=pltpu.CompilerParams(vmem_limit_bytes=6 * 2**20),
    )(
        pltpu.with_memory_space_constraint(lamb, pltpu.VMEM),
        pltpu.with_memory_space_constraint(peak, pltpu.VMEM),
    )
    return out, top[0, 0]


def solution(mesh):
    placed = (P(None, "gy", "pa", None), P("gy"))
    return jax.shard_map(
        body,
        mesh=mesh,
        in_specs=placed,
        out_specs=(P(None, "gy", "pa", None), P()),
        check_vma=False,
    )
```
